512 devices in a mesh: row: 32 (over x, y, core), col: 16 (over z).
Axes of the slice: x: 4, y: 4, z: 16, core: 2. Of those that a mesh axis runs over, the one named last changes fastest.
Arguments:
- z_anc: float32 [8192, 8192], P('row', 'col'), may hold values from -0.5 to 0.5
- in_one: int32 [64], replicated, may hold values from 0 to 1
- in_two: int32 [64], replicated, may hold values from 0 to 1, as said below
- l_one: float32 [8192, 512], P(('row', 'col')), may hold values from -0.015625 to 0.015625
- l_two: float32 [8192, 512], P(('row', 'col')), may hold values from -0.015625 to 0.015625
- l_pair: float32 [512, 512], P('row'), may hold values from -0.25 to 0.25
- linv_one: float32 [512, 512], replicated, as said below
- linv_two: float32 [512, 512], replicated, as said below
Outputs:
- col_one: float32 [8192, 512], P(('row', 'col'))
- diag_one: float32 [512, 512], P('row', 'col')
- col_two: float32 [8192, 512], P(('row', 'col'))
- pair_block: float32 [512, 512], P('row', 'col')
- diag_two: float32 [512, 512], P('row', 'col')
The draws below stay inside these ranges and needn't reach their ends.
Inputs may be any that keep to these rules, and one draw needn't show every extreme that they name: `in_two`: a block in the second supernode's ancestor structure is also in the first supernode's structure. `linv_one`: lower triangular, diagonal between 0.5 and 1.5. `linv_two`: lower triangular, diagonal between 0.5 and 1.5.
All inputs are finite; a program needn't handle non-finite values.
Results may differ from the reference program's by a relative error of at most 0.00003.
Values sent between devices are 32-bit elements; how exact they have to be, the bound alone decides.
A program may use at most 64 MiB of HBM per device.

```python
from functools import partial
import jax
import jax.numpy as jnp
from jax import lax

W = 512
BLK = 128
NDOF = 8192
NBLK = 64


def flag_pair(key):
    first = jax.random.randint(jax.random.fold_in(key, 11), (NBLK,), 0, 2)
    second = jax.random.randint(jax.random.fold_in(key, 12), (NBLK,), 0, 2)
    return (first, first * second)


def triangle(key):
    below = jax.random.normal(jax.random.fold_in(key, 21), (W, W), jnp.float32) * (0.5 * W ** (-0.5))
    diag_vals = jax.random.uniform(jax.random.fold_in(key, 22), (W,), jnp.float32, 0.5, 1.5)
    rows = jnp.arange(W)[:, None]
    cols = jnp.arange(W)[None, :]
    return jnp.where(rows > cols, below, 0.0) + jnp.where(rows == cols, diag_vals[:, None], 0.0)


def draw_in_one(key, part):
    shared = flag_pair(key)
    return shared[0].astype(jnp.int32)


def draw_in_two(key, part):
    shared = flag_pair(key)
    return shared[1].astype(jnp.int32)


def draw_linv_one(key, part):
    key = jax.random.fold_in(key, 3)
    return triangle(key).astype(jnp.float32)


def draw_linv_two(key, part):
    key = jax.random.fold_in(key, 4)
    return triangle(key).astype(jnp.float32)


def raised(values, key, source, target, blocks, factor):
    def block_of(position):
        return (jnp.arange(values.shape[position]) // (values.shape[position] // blocks)).reshape((-1,) + (1,) * (values.ndim - 1 - position))

    first = jax.random.permutation(key, blocks)[block_of(target)]
    far = (block_of(target) + blocks // 2) % blocks
    return jnp.where((block_of(source) == first) | (block_of(source) == far), factor * values, values)


def level_of(own_key, dims, shards, smallest, high):
    gain = 1.0
    for dim, shards_of in shards:
        heights = jax.random.uniform(jax.random.fold_in(jax.random.fold_in(own_key, 6), dim), (shards_of,), jnp.float32, smallest / len(shards), high / len(shards))
        gain = gain * jnp.repeat(jnp.exp(heights), dims[dim] // shards_of).reshape((-1,) + (1,) * (len(dims) - 1 - dim))
    return gain


def centred(key, dims, deviation, limit, cuts=(), dtype=jnp.bfloat16):
    drawn = jax.random.normal(key, dims, jnp.float32) * deviation
    if len(cuts) > 0:
        drawn = level_of(key, dims, cuts, -0.22, 0.18) * drawn
    return jnp.clip(drawn, min=-limit, max=limit).astype(dtype)


def noise_with(rng, extent, deviation, most, shards, heavy, held_as=jnp.bfloat16):
    values = deviation * jax.random.normal(rng, extent, jnp.float32)
    if shards:
        values = values * level_of(rng, extent, shards, -0.22, 0.18)
    return jnp.clip(raised(values, jax.random.fold_in(rng, 3), *heavy), -most, most).astype(held_as)


def setup_inputs(seed: int = 0) -> dict:
    arg_keys = jax.random.split(jax.random.key(seed), 9)
    return {
        "z_anc": noise_with(arg_keys[0], (NDOF, NDOF), (4 * NDOF ** -0.5), 0.5, ((0, 32), (1, 16)), (1, 0, 32, 2.75), jnp.float32),
        "in_one": draw_in_one(jax.random.fold_in(arg_keys[8], 71), 0),
        "in_two": draw_in_two(jax.random.fold_in(arg_keys[8], 71), 0),
        "l_one": centred(arg_keys[3], (NDOF, W), (256 * W) ** -0.5, 0.015625, ((0, 512),), jnp.float32),
        "l_two": centred(arg_keys[4], (NDOF, W), (256 * W) ** -0.5, 0.015625, ((0, 512),), jnp.float32),
        "l_pair": centred(arg_keys[5], (W, W), W ** -0.5, 0.25, ((0, 32),), jnp.float32),
        "linv_one": draw_linv_one(jax.random.fold_in(arg_keys[8], 71), 0),
        "linv_two": draw_linv_two(jax.random.fold_in(arg_keys[8], 71), 0),
    }


def row_flags(flags):
    return jnp.repeat(flags.astype(jnp.float32), BLK)


def reference(z_anc, in_one, in_two, l_one, l_two, l_pair, linv_one, linv_two):
    highest = lax.Precision.HIGHEST
    product = partial(jnp.dot, precision=highest, preferred_element_type=jnp.float32)
    mask_one = row_flags(in_one)[:, None]
    mask_two = row_flags(in_two)[:, None]
    u_one = mask_one * product(l_one, linv_one)
    u_two = mask_two * product(l_two, linv_two)
    u_pair = product(l_pair, linv_two)
    y_one = product(z_anc, u_one)
    col_one = -(mask_one * y_one)
    diag_one = product(linv_one.T, linv_one) + product(u_one.T, y_one)
    y_two = product(z_anc, u_two) + product(col_one, u_pair)
    y_pair = product(col_one.T, u_two) + product(diag_one, u_pair)
    col_two = -(mask_two * y_two)
    pair_block = -y_pair
    diag_two = product(linv_two.T, linv_two) + product(u_two.T, y_two) + product(u_pair.T, y_pair)
    return col_one, diag_one, col_two, pair_block, diag_two
```

```python
import functools

import jax
import jax.numpy as jnp
from jax import lax
from jax.experimental import pallas as pl
from jax.experimental.pallas import tpu as pltpu
from jax.sharding import PartitionSpec as P

BLK = 128
FINE = 16
MESH = pl.DeviceIdType.MESH
F32 = jnp.float32
BF16 = jnp.bfloat16


def split(value):
    high = value.astype(BF16)
    low = (value - high.astype(F32)).astype(BF16)
    return high, low


def dot_parts(a, b, dims):
    def one(left, right):
        return lax.dot_general(left, right, (dims, ((), ())), preferred_element_type=F32)

    return one(a[0], b[0]) + (one(a[0], b[1]) + one(a[1], b[0]))


def nn(a, b):
    return dot_parts(split(a), b, ((1,), (0,)))


def nt(a, b):
    return dot_parts(split(a), b, ((1,), (1,)))


def kernel(
    side,
    in_one, in_two, l_one, l_two, l_pair, z_hbm, linv_one_hbm, linv_two_hbm,
    col_one, diag_one, col_two, pair_block, diag_two,
    z_v, linv_one, linv_two, own, hop, far, near, res, m_high, m_low, part, ring, pack, got,
    local_sem, hop_recv, far_recv, send_sem, first_recv, second_recv, core_recv, ring_send, ring_recv, got_sem,
):
    chips = side * side
    zn = chips
    width = l_one.shape[1]
    row = lax.axis_index("row")
    col = lax.axis_index("col")
    core = lax.rem(row, 2)
    chip = lax.div(row, 2)
    x = lax.div(chip, side)
    y = lax.rem(chip, side)
    sibling = row + 1 - 2 * core

    def local(source, target, sem):
        return pltpu.make_async_copy(source, target, sem)

    def send(source, target, s_sem, r_sem, device):
        pltpu.make_async_remote_copy(
            src_ref=source, dst_ref=target, send_sem=s_sem, recv_sem=r_sem,
            device_id=device, device_id_type=MESH,
        ).start()

    def arrived(ref, sem):
        pltpu.make_async_copy(ref, ref, sem).wait()

    staged = [
        local(z_hbm, z_v, local_sem.at[0]),
        local(linv_one_hbm, linv_one, local_sem.at[1]),
        local(linv_two_hbm, linv_two, local_sem.at[2]),
    ]
    for copy in staged:
        copy.start()

    barrier = pltpu.get_barrier_semaphore()

    def greet(device):
        pl.semaphore_signal(barrier, inc=1, device_id=device, device_id_type=MESH)

    greet((sibling, col))
    for step in range(1, chips):
        greet((2 * lax.rem(chip + step, chips) + core, col))
    for step in range(1, zn):
        greet((row, lax.rem(col + step, zn)))

    block = lax.div(row * (zn * FINE) + col * FINE, BLK)
    flag_one = in_one[block].astype(F32)
    flag_two = in_two[block].astype(F32)
    mine_one = l_one[...] * flag_one
    mine_two = l_two[...] * flag_two
    here = core * chips + chip
    near[here, :, :width] = mine_one
    near[here, :, width:2 * width] = mine_two
    near[here, :, 2 * width:] = l_pair[...]
    tiles = width // 128
    for tile in range(2 * tiles):
        source = mine_one if tile < tiles else mine_two
        at = (tile % tiles) * 128
        for half in range(2):
            own[2 * tile + half] = source[8 * half:8 * half + 8, at:at + 128]

    pl.semaphore_wait(barrier, chips + zn - 1)

    mine = local(own.at[chip], hop.at[chip], hop_recv.at[chip])
    mine.start()
    for step in range(1, chips):
        to = lax.rem(chip + step, chips)
        send(own.at[to], hop.at[chip], send_sem.at[0], hop_recv.at[chip], (2 * to + core, col))
    for step in range(1, zn):
        to = lax.rem(col + step, zn)
        arrived(hop.at[to], hop_recv.at[to])
        send(hop.at[to], far.at[here, col], send_sem.at[1], far_recv, (row, to))
    arrived(hop.at[col], hop_recv.at[col])
    far[here, col] = hop[col]

    def place(first, second, which):
        xs = lax.rem(x + side + first * (1 - which) + second * which, side)
        ys = lax.rem(y + side + first * which + second * (1 - which), side)
        return xs * side + ys

    def peer(first, second):
        return (2 * place(first, second, core) + core, col)

    def spread_first(buf, which):
        for d in range(1, side):
            send(buf.at[here], buf.at[here], send_sem.at[2 + which], first_recv.at[which, d], peer(d, 0))

    def spread_second(buf, which):
        for e in range(side):
            spot = core * chips + place(-e, 0, core)
            if e:
                arrived(buf.at[spot], first_recv.at[which, e])
            for d in range(1, side):
                send(buf.at[spot], buf.at[spot], send_sem.at[2 + which], second_recv.at[which, e, d], peer(0, d))
            send(buf.at[spot], buf.at[spot], send_sem.at[2 + which], core_recv.at[which], (sibling, col))

    def spread_third(buf, which):
        for d in range(1, side):
            for e in range(side):
                spot = core * chips + place(-e, -d, core)
                arrived(buf.at[spot], second_recv.at[which, e, d])
                send(buf.at[spot], buf.at[spot], send_sem.at[2 + which], core_recv.at[which], (sibling, col))

    def spread_end(buf, which):
        arrived(buf.at[pl.ds((1 - core) * chips, chips)], core_recv.at[which])

    staged[0].wait()
    z_parts = split(z_v[...])
    arrived(far.at[0, pl.ds(0, zn - 1)], far_recv)
    spread_first(far, 0)
    spread_second(far, 0)
    spread_third(far, 0)
    spread_end(far, 0)
    spread_first(near, 1)

    for which in range(2):
        for tile in range(2 * tiles):
            at = which * chips + 2 * tile
            value = jnp.stack([far[at], far[at + 1]], axis=1).reshape(zn * FINE, 128)
            high, low = split(value)
            rows = slice(which * zn * FINE, (which + 1) * zn * FINE)
            m_high[rows, tile * 128:tile * 128 + 128] = high
            m_low[rows, tile * 128:tile * 128 + 128] = low

    most = zn // 2
    steps = ((most, most - 1), (most - 1, most))
    up = lax.rem(col + 1, zn)
    down = lax.rem(col + zn - 1, zn)

    def ring_step(half, way, step):
        count = steps[half][way]
        if step >= count:
            return
        owner = lax.rem(col + zn + (count - step if way == 0 else step - count), zn)
        if step == 0:
            source = part.at[half, owner]
        else:
            source = ring.at[half, way, step - 1]
            arrived(source, ring_recv.at[half, way, step - 1])
            ring[half, way, step - 1] = ring[half, way, step - 1] + part[half, owner]
        send(source, ring.at[half, way, step], ring_send.at[half, way], ring_recv.at[half, way, step],
             (row, up if way == 0 else down))

    for half in range(2):
        cols = slice(half * width, (half + 1) * width)
        product = dot_parts(z_parts, (m_high[:, cols], m_low[:, cols]), ((1,), (0,)))
        part[half] = product.reshape(zn, FINE, width)
        for way in range(2):
            ring_step(half, way, 0)

    for step in range(1, most):
        for half in range(2):
            for way in range(2):
                ring_step(half, way, step)
        if step == min(2, most - 1):
            spread_second(near, 1)
        if step == min(4, most - 1):
            spread_third(near, 1)

    staged[1].wait()
    staged[2].wait()
    inv_one = split(linv_one[...])
    inv_two = split(linv_two[...])
    spread_end(near, 1)
    count = 2 * chips * FINE
    near_one = split(near[:, :, :width].reshape(count, width))
    near_two = split(near[:, :, width:2 * width].reshape(count, width))
    pair = jnp.concatenate(
        [near[which * chips + t, :, 2 * width:] for t in range(chips) for which in range(2)], axis=0
    )
    pair = split(pair)
    line = lax.broadcasted_iota(jnp.int32, (48, width), 0)
    lane = lax.broadcasted_iota(jnp.int32, (48, width), 1)
    wanted = jnp.where(line < 16, row * 16 + line, col * 32 + line - 16)
    pick = jnp.where(lane == wanted, 1.0, 0.0).astype(F32)
    tri_one = nt(pick, inv_one)
    tri_two = nt(pick, inv_two)
    tri_pair = nt(nt(tri_two, pair), inv_one)
    u_one_t = nt(tri_one[:16], near_one)
    u_two_t = nt(tri_two[:16], near_two)
    q_t = nt(tri_pair[:16], near_one)
    gram_one = nt(tri_one[:16], split(tri_one[16:]))
    gram_pair = nt(tri_one[:16], split(tri_pair[16:]))
    gram_two = nt(tri_two[:16], split(tri_two[16:])) + nt(tri_pair[:16], split(tri_pair[16:]))

    for half in range(2):
        ends = []
        for way in range(2):
            last = steps[half][way] - 1
            arrived(ring.at[half, way, last], ring_recv.at[half, way, last])
            ends.append(ring[half, way, last])
        res[here, :, half * width:(half + 1) * width] = part[half, col] + ends[0] + ends[1]

    spread_first(res, 2)
    y_one = nn(res[here, :, :width], inv_one)
    one = -(flag_one * y_one)
    col_one[...] = one
    spread_second(res, 2)
    y_two = nn(res[here, :, width:] + nn(one, pair), inv_two)
    col_two[...] = -(flag_two * y_two)
    spread_third(res, 2)
    spread_end(res, 2)

    res_one = split(res[:, :, :width].reshape(count, width))
    res_two = split(res[:, :, width:].reshape(count, width))
    a = nn(jnp.concatenate([u_one_t, u_two_t, q_t], axis=0), res_one)
    b = nn(u_two_t, res_two)
    y_t = nt(jnp.concatenate([tri_one[:16], tri_pair[:16]], axis=0), res_one)
    c = nn(y_t, near_two)
    d = nn(jnp.concatenate([a[:16], a[32:] - a[16:32]], axis=0), inv_one)
    e = nn(d, pair) + jnp.concatenate([-c[:16], b - c[16:]], axis=0)
    s = nn(e, inv_two)
    sums = (d[:16], s[:16], s[16:])

    lanes = lax.broadcasted_iota(jnp.int32, (FINE, 128), 1)
    for owner in range(zn):
        at = (owner // 4) * 128
        packed = jnp.zeros((FINE, 128), F32)
        for n in range(3):
            piece = sums[n][:, at:at + 128]
            shift = (32 * n - 32 * (owner % 4)) % 128
            if shift:
                piece = pltpu.roll(piece, shift, 1)
            packed = jnp.where((lanes >= 32 * n) & (lanes < 32 * n + 32), piece, packed)
        pack[owner] = packed
    for step in range(1, zn):
        to = lax.rem(col + step, zn)
        send(pack.at[to], got.at[step], got_sem.at[0], got_sem.at[1], (row, to))
    arrived(got.at[pl.ds(1, zn - 1)], got_sem.at[1])
    total = pack[col]
    for step in range(1, zn):
        total = total + got[step]
    diag_one[...] = total[:, :32] + gram_one
    pair_block[...] = -(pltpu.roll(total, 96, 1)[:, :32] + gram_pair)
    diag_two[...] = pltpu.roll(total, 64, 1)[:, :32] + gram_two

    arrived(own.at[pl.ds(0, chips - 1)], send_sem.at[0])
    arrived(hop.at[pl.ds(0, zn - 1)], send_sem.at[1])
    for which, buf in enumerate((far, near, res)):
        arrived(buf.at[pl.ds(0, 2 * chips - 1)], send_sem.at[2 + which])
    for half in range(2):
        for way in range(2):
            arrived(part.at[half, pl.ds(0, steps[half][way])], ring_send.at[half, way])
    arrived(got.at[pl.ds(1, zn - 1)], got_sem.at[0])


def shards(side, z_anc, in_one, in_two, l_one, l_two, l_pair, linv_one, linv_two):
    width = l_one.shape[1]
    chips = side * side
    zn = chips
    rows, depth = z_anc.shape
    vmem = pl.BlockSpec(memory_space=pltpu.VMEM)
    smem = pl.BlockSpec(memory_space=pltpu.SMEM)
    hbm = pl.BlockSpec(memory_space=pl.ANY)
    dma = pltpu.SemaphoreType.DMA
    out = lambda *shape: jax.ShapeDtypeStruct(shape, F32)
    return tuple(pl.pallas_call(
        functools.partial(kernel, side),
        out_shape=(
            out(FINE, width), out(16, 32), out(FINE, width), out(16, 32), out(16, 32),
        ),
        in_specs=[smem, smem, vmem, vmem, vmem, hbm, hbm, hbm],
        out_specs=[vmem] * 5,
        scratch_shapes=[
            pltpu.VMEM((rows, depth), F32),
            pltpu.VMEM((width, width), F32),
            pltpu.VMEM((width, width), F32),
            pltpu.VMEM((chips, 8, 128), F32),
            pltpu.VMEM((chips, 8, 128), F32),
            pltpu.VMEM((2 * chips, zn, 8, 128), F32),
            pltpu.VMEM((2 * chips, FINE, 3 * width), F32),
            pltpu.VMEM((2 * chips, FINE, 2 * width), F32),
            pltpu.VMEM((depth, 2 * width), BF16),
            pltpu.VMEM((depth, 2 * width), BF16),
            pltpu.VMEM((2, zn, FINE, width), F32),
            pltpu.VMEM((2, 2, zn // 2, FINE, width), F32),
            pltpu.VMEM((zn, FINE, 128), F32),
            pltpu.VMEM((zn, FINE, 128), F32),
            dma((3,)),
            dma((chips,)),
            dma,
            dma((5,)),
            dma((3, side)),
            dma((3, side, side)),
            dma((3,)),
            dma((2, 2)),
            dma((2, 2, zn // 2)),
            dma((2,)),
        ],
        compiler_params=pltpu.CompilerParams(
            collective_id=0, has_side_effects=True, vmem_limit_bytes=48 * 1024 * 1024
        ),
    )(in_one, in_two, l_one, l_two, l_pair, z_anc, linv_one, linv_two))


def solution(mesh):
    side = 1
    while side * side < mesh.shape["col"]:
        side += 1
    placed = (
        P("row", "col"),
        P(),
        P(),
        P(("row", "col"), None),
        P(("row", "col"), None),
        P("row", None),
        P(),
        P(),
    )
    return jax.shard_map(
        functools.partial(shards, side),
        mesh=mesh,
        in_specs=placed,
        out_specs=(
            P(("row", "col"), None),
            P("row", "col"),
            P(("row", "col"), None),
            P("row", "col"),
            P("row", "col"),
        ),
        check_vma=False,
    )
```

```python
import functools

import jax
import jax.numpy as jnp
from jax import lax
from jax.experimental import pallas as pl
from jax.experimental.pallas import tpu as pltpu
from jax.sharding import PartitionSpec as P

BLK = 128
FINE = 16
MESH = pl.DeviceIdType.MESH
F32 = jnp.float32
BF16 = jnp.bfloat16


def split(value):
    high = value.astype(BF16)
    low = (value - high.astype(F32)).astype(BF16)
    return high, low


def dot_parts(a, b, dims):
    def one(left, right):
        return lax.dot_general(left, right, (dims, ((), ())), preferred_element_type=F32)

    return one(a[0], b[0]) + (one(a[0], b[1]) + one(a[1], b[0]))


def nn(a, b):
    return dot_parts(split(a), b, ((1,), (0,)))


def nt(a, b):
    return dot_parts(split(a), b, ((1,), (1,)))


def kernel(
    side, pieces,
    in_one_hbm, in_two_hbm, l_one_hbm, l_two_hbm, l_pair_hbm, z_hbm, linv_one_hbm, linv_two_hbm,
    col_one, diag_one, col_two, pair_block, diag_two,
    in_one, in_two, l_one, l_two, l_pair, z_v, linv_one, linv_two,
    own, hop, far, near, res, m_high, m_low, part, even, odd, pack, got,
    local_sem, hop_recv, far_recv, send_sem, first_recv, second_recv, core_recv, tree_send, even_recv, odd_recv, got_sem,
):
    chips = side * side
    zn = chips
    width = l_one.shape[1]
    row = lax.axis_index("row")
    col = lax.axis_index("col")
    core = lax.rem(row, 2)
    chip = lax.div(row, 2)
    x = lax.div(chip, side)
    y = lax.rem(chip, side)
    sibling = row + 1 - 2 * core
    here = core * chips + chip

    def send(source, target, s_sem, r_sem, device):
        pltpu.make_async_remote_copy(
            src_ref=source, dst_ref=target, send_sem=s_sem, recv_sem=r_sem,
            device_id=device, device_id_type=MESH,
        ).start()

    def arrived(ref, sem):
        pltpu.make_async_copy(ref, ref, sem).wait()

    staged = [
        pltpu.make_async_copy(source, target, local_sem.at[n])
        for n, (source, target) in enumerate((
            (in_one_hbm, in_one), (in_two_hbm, in_two), (l_one_hbm, l_one), (l_two_hbm, l_two),
            (l_pair_hbm, l_pair), (z_hbm, z_v), (linv_one_hbm, linv_one), (linv_two_hbm, linv_two),
        ))
    ]
    for copy in staged:
        copy.start()

    barrier = pltpu.get_barrier_semaphore()

    def greet(device):
        pl.semaphore_signal(barrier, inc=1, device_id=device, device_id_type=MESH)

    for step in sorted(range(1, zn), key=lambda n: -min(n, zn - n)):
        greet((row, lax.rem(col + step, zn)))
    for step in range(1, chips):
        greet((2 * lax.rem(chip + step, chips) + core, col))
    greet((sibling, col))

    for copy in staged[:5]:
        copy.wait()
    block = lax.div(row * (zn * FINE) + col * FINE, BLK)
    flag_one = in_one[block].astype(F32)
    flag_two = in_two[block].astype(F32)
    mine_one = l_one[...] * flag_one
    mine_two = l_two[...] * flag_two
    near[here, :, :width] = mine_one
    near[here, :, width:2 * width] = mine_two
    near[here, :, 2 * width:] = l_pair[...]
    tiles = width // 128
    for tile in range(2 * tiles):
        source = mine_one if tile < tiles else mine_two
        at = (tile % tiles) * 128
        for half in range(2):
            own[2 * tile + half] = source[8 * half:8 * half + 8, at:at + 128]

    group = zn // 2
    lead = zn // 4
    staged[5].wait()
    turn = lax.rem(lead * FINE + (zn - col) * FINE, zn * FINE)
    depth = zn * FINE
    z_parts = split(jnp.concatenate(
        [pltpu.roll(z_v[:, n * depth:(n + 1) * depth], turn, 1) for n in range(2)], axis=1
    ))

    pl.semaphore_wait(barrier, chips + zn - 1)

    mine = pltpu.make_async_copy(own.at[chip], hop.at[chip], hop_recv.at[chip])
    mine.start()
    for step in range(1, chips):
        to = lax.rem(chip + step, chips)
        send(own.at[to], hop.at[chip], send_sem.at[0], hop_recv.at[chip], (2 * to + core, col))
    for step in sorted(range(1, zn), key=lambda n: -min(n, zn - n)):
        to = lax.rem(col + step, zn)
        spot = (lead - step) % zn
        arrived(hop.at[to], hop_recv.at[to])
        send(hop.at[to], far.at[here, spot], send_sem.at[1], far_recv.at[spot // group], (row, to))
    arrived(hop.at[col], hop_recv.at[col])
    far[here, lead] = hop[col]

    def place(first, second, which):
        xs = lax.rem(x + side + first * (1 - which) + second * which, side)
        ys = lax.rem(y + side + first * which + second * (1 - which), side)
        return xs * side + ys

    def peer(first, second):
        return (2 * place(first, second, core) + core, col)

    def spread_first(view, sem, which):
        for d in range(1, side):
            send(view(here), view(here), send_sem.at[sem], first_recv.at[which, d], peer(d, 0))

    def spread_second(view, sem, which):
        for e in range(side):
            spot = core * chips + place(-e, 0, core)
            if e:
                arrived(view(spot), first_recv.at[which, e])
            for d in range(1, side):
                send(view(spot), view(spot), send_sem.at[sem], second_recv.at[which, e, d], peer(0, d))
            send(view(spot), view(spot), send_sem.at[sem], core_recv.at[which], (sibling, col))

    def spread_third(view, sem, which):
        for d in range(1, side):
            for e in range(side):
                spot = core * chips + place(-e, -d, core)
                arrived(view(spot), second_recv.at[which, e, d])
                send(view(spot), view(spot), send_sem.at[sem], core_recv.at[which], (sibling, col))

    def spread_end(view, which):
        arrived(view(pl.ds((1 - core) * chips, chips)), core_recv.at[which])

    def far_half(n):
        return lambda spot: far.at[spot, pl.ds(n * group, group)]

    def near_all(spot):
        return near.at[spot]

    def res_half(n):
        return lambda spot: res.at[n, spot]

    arrived(far.at[0, pl.ds(0, group - 1)], far_recv.at[0])
    spread_first(far_half(0), 2, 0)
    arrived(far.at[0, pl.ds(0, group)], far_recv.at[1])
    spread_first(far_half(1), 2, 1)
    spread_second(far_half(0), 2, 0)
    spread_second(far_half(1), 2, 1)
    spread_third(far_half(0), 2, 0)
    spread_third(far_half(1), 2, 1)
    spread_end(far_half(0), 0)
    spread_end(far_half(1), 1)
    spread_first(near_all, 3, 2)

    for which in range(2):
        for tile in range(2 * tiles):
            at = which * chips + 2 * tile
            value = jnp.stack([far[at], far[at + 1]], axis=1).reshape(depth, 128)
            high, low = split(value)
            rows = slice(which * depth, (which + 1) * depth)
            m_high[rows, tile * 128:tile * 128 + 128] = high
            m_low[rows, tile * 128:tile * 128 + 128] = low

    most = zn // 2
    ways = (0, 1)

    def reach(piece, way):
        return most if (piece + way) % 2 == 0 else most - 1

    def along(way, distance):
        return lax.rem(col + (distance if way == 0 else zn - distance), zn)

    def leaf(piece, way, distance):
        if distance > reach(piece, way):
            return
        source = part.at[piece, along(way, distance)]
        level = (distance - 1) // 2
        if distance % 2:
            send(source, odd.at[piece, way, level], tree_send.at[piece, way], odd_recv.at[piece, way, level],
                 (row, along(way, 1)))
        else:
            send(source, even.at[piece, way, level], tree_send.at[piece, way], even_recv.at[piece, way, level],
                 (row, along(way, 2)))

    def gathered(piece, way, distance):
        level = distance // 2
        arrived(odd.at[piece, way, level], odd_recv.at[piece, way, level])
        total = odd[piece, way, level]
        if distance + 2 <= reach(piece, way):
            arrived(even.at[piece, way, level], even_recv.at[piece, way, level])
            total = total + even[piece, way, level]
        return total

    def chain(piece, way, distance):
        if distance + 1 > reach(piece, way):
            leaf(piece, way, distance)
            return
        level = distance // 2
        odd[piece, way, level] = part[piece, along(way, distance)] + gathered(piece, way, distance)
        send(odd.at[piece, way, level], even.at[piece, way, level - 1], tree_send.at[piece, way],
             even_recv.at[piece, way, level - 1], (row, along(way, 2)))

    share = 2 * width // pieces
    for piece in range(pieces):
        cols = slice(piece * share, (piece + 1) * share)
        product = dot_parts(z_parts, (m_high[:, cols], m_low[:, cols]), ((1,), (0,)))
        part[piece] = product.reshape(zn, FINE, share)
        for way in ways:
            leaf(piece, way, most)
            leaf(piece, way, most - 1)
    if most > 3:
        for piece in range(pieces):
            for way in ways:
                leaf(piece, way, most - 3)

    for distance in range(most - 2, 0, -2):
        for piece in range(pieces):
            for way in ways:
                chain(piece, way, distance)
        if distance > 3:
            for piece in range(pieces):
                for way in ways:
                    leaf(piece, way, distance - 3)
        if distance == most - 2:
            spread_second(near_all, 3, 2)
        if distance == max(most - 4, 2):
            spread_third(near_all, 3, 2)
    if most <= 2:
        spread_second(near_all, 3, 2)
        spread_third(near_all, 3, 2)

    for copy in staged[6:]:
        copy.wait()
    inv_one = split(linv_one[...])
    inv_two = split(linv_two[...])
    spread_end(near_all, 2)
    count = 2 * chips * FINE
    near_one = split(near[:, :, :width].reshape(count, width))
    near_two = split(near[:, :, width:2 * width].reshape(count, width))
    pair = jnp.concatenate(
        [near[which * chips + t, :, 2 * width:] for t in range(chips) for which in range(2)], axis=0
    )
    pair = split(pair)
    line = lax.broadcasted_iota(jnp.int32, (48, width), 0)
    lane = lax.broadcasted_iota(jnp.int32, (48, width), 1)
    wanted = jnp.where(line < 16, row * 16 + line, col * 32 + line - 16)
    pick = jnp.where(lane == wanted, 1.0, 0.0).astype(F32)
    tri_one = nt(pick, inv_one)
    tri_two = nt(pick, inv_two)
    tri_pair = nt(nt(tri_two, pair), inv_one)
    u_one_t = nt(tri_one[:16], near_one)
    u_two_t = nt(tri_two[:16], near_two)
    q_t = nt(tri_pair[:16], near_one)
    gram_one = nt(tri_one[:16], split(tri_one[16:]))
    gram_pair = nt(tri_one[:16], split(tri_pair[16:]))
    gram_two = nt(tri_two[:16], split(tri_two[16:])) + nt(tri_pair[:16], split(tri_pair[16:]))

    for piece in range(pieces):
        sums = [gathered(piece, way, 0) for way in ways]
        at = piece * share % width
        n = piece * share // width
        res[n, here, :, at:at + share] = part[piece, col] + sums[0] + sums[1]
        if at + share == width:
            spread_first(res_half(n), 4, 3 + n)

    y_one = nn(res[0, here], inv_one)
    one = -(flag_one * y_one)
    col_one[...] = one
    spread_second(res_half(0), 4, 3)
    spread_second(res_half(1), 4, 4)
    y_two = nn(res[1, here] + nn(one, pair), inv_two)
    col_two[...] = -(flag_two * y_two)
    spread_third(res_half(0), 4, 3)
    spread_third(res_half(1), 4, 4)
    spread_end(res_half(0), 3)

    res_one = split(res[0].reshape(count, width))
    a = nn(jnp.concatenate([u_one_t, u_two_t, q_t], axis=0), res_one)
    y_t = nt(jnp.concatenate([tri_one[:16], tri_pair[:16]], axis=0), res_one)
    c = nn(y_t, near_two)
    d = nn(jnp.concatenate([a[:16], a[32:] - a[16:32]], axis=0), inv_one)
    e = nn(d, pair)
    spread_end(res_half(1), 4)
    b = nn(u_two_t, split(res[1].reshape(count, width)))
    s = nn(e + jnp.concatenate([-c[:16], b - c[16:]], axis=0), inv_two)
    sums = (d[:16], s[:16], s[16:])

    lanes = lax.broadcasted_iota(jnp.int32, (FINE, 128), 1)
    for owner in range(zn):
        at = (owner // 4) * 128
        packed = jnp.zeros((FINE, 128), F32)
        for n in range(3):
            piece = sums[n][:, at:at + 128]
            shift = (32 * n - 32 * (owner % 4)) % 128
            if shift:
                piece = pltpu.roll(piece, shift, 1)
            packed = jnp.where((lanes >= 32 * n) & (lanes < 32 * n + 32), piece, packed)
        pack[owner] = packed
    for step in sorted(range(1, zn), key=lambda n: -min(n, zn - n)):
        to = lax.rem(col + step, zn)
        send(pack.at[to], got.at[step], got_sem.at[0], got_sem.at[1], (row, to))
    arrived(got.at[pl.ds(1, zn - 1)], got_sem.at[1])
    total = pack[col]
    for step in range(1, zn):
        total = total + got[step]
    diag_one[...] = total[:, :32] + gram_one
    pair_block[...] = -(pltpu.roll(total, 96, 1)[:, :32] + gram_pair)
    diag_two[...] = pltpu.roll(total, 64, 1)[:, :32] + gram_two

    arrived(own.at[pl.ds(0, chips - 1)], send_sem.at[0])
    arrived(hop.at[pl.ds(0, zn - 1)], send_sem.at[1])
    arrived(far.at[pl.ds(0, 2 * chips - 1)], send_sem.at[2])
    arrived(near.at[pl.ds(0, 2 * chips - 1)], send_sem.at[3])
    for n in range(2):
        arrived(res.at[n, pl.ds(0, 2 * chips - 1)], send_sem.at[4])
    for piece in range(pieces):
        for way in ways:
            arrived(part.at[piece, pl.ds(0, reach(piece, way))], tree_send.at[piece, way])
    arrived(got.at[pl.ds(1, zn - 1)], got_sem.at[0])


def shards(side, z_anc, in_one, in_two, l_one, l_two, l_pair, linv_one, linv_two):
    width = l_one.shape[1]
    chips = side * side
    zn = chips
    rows, depth = z_anc.shape
    pieces = 4 if width > 128 else 2
    share = 2 * width // pieces
    levels = zn // 4
    vmem = pl.BlockSpec(memory_space=pltpu.VMEM)
    hbm = pl.BlockSpec(memory_space=pl.ANY)
    dma = pltpu.SemaphoreType.DMA
    out = lambda *shape: jax.ShapeDtypeStruct(shape, F32)
    held = lambda array: pltpu.VMEM(array.shape, array.dtype)
    return tuple(pl.pallas_call(
        functools.partial(kernel, side, pieces),
        out_shape=(
            out(FINE, width), out(16, 32), out(FINE, width), out(16, 32), out(16, 32),
        ),
        in_specs=[hbm] * 8,
        out_specs=[vmem] * 5,
        scratch_shapes=[
            pltpu.SMEM(in_one.shape, in_one.dtype),
            pltpu.SMEM(in_two.shape, in_two.dtype),
            held(l_one), held(l_two), held(l_pair), held(z_anc), held(linv_one), held(linv_two),
            pltpu.VMEM((chips, 8, 128), F32),
            pltpu.VMEM((chips, 8, 128), F32),
            pltpu.VMEM((2 * chips, zn, 8, 128), F32),
            pltpu.VMEM((2 * chips, FINE, 3 * width), F32),
            pltpu.VMEM((2, 2 * chips, FINE, width), F32),
            pltpu.VMEM((depth, 2 * width), BF16),
            pltpu.VMEM((depth, 2 * width), BF16),
            pltpu.VMEM((pieces, zn, FINE, share), F32),
            pltpu.VMEM((pieces, 2, levels, FINE, share), F32),
            pltpu.VMEM((pieces, 2, levels, FINE, share), F32),
            pltpu.VMEM((zn, FINE, 128), F32),
            pltpu.VMEM((zn, FINE, 128), F32),
            dma((8,)),
            dma((chips,)),
            dma((2,)),
            dma((5,)),
            dma((5, side)),
            dma((5, side, side)),
            dma((5,)),
            dma((pieces, 2)),
            dma((pieces, 2, levels)),
            dma((pieces, 2, levels)),
            dma((2,)),
        ],
        compiler_params=pltpu.CompilerParams(
            collective_id=0, has_side_effects=True, vmem_limit_bytes=63 * 1024 * 1024
        ),
    )(in_one, in_two, l_one, l_two, l_pair, z_anc, linv_one, linv_two))


def solution(mesh):
    side = 1
    while side * side < mesh.shape["col"]:
        side += 1
    placed = (
        P("row", "col"),
        P(),
        P(),
        P(("row", "col"), None),
        P(("row", "col"), None),
        P("row", None),
        P(),
        P(),
    )
    return jax.shard_map(
        functools.partial(shards, side),
        mesh=mesh,
        in_specs=placed,
        out_specs=(
            P(("row", "col"), None),
            P("row", "col"),
            P(("row", "col"), None),
            P("row", "col"),
            P("row", "col"),
        ),
        check_vma=False,
    )
```

```python
import functools

import jax
import jax.numpy as jnp
from jax import lax
from jax.experimental import pallas as pl
from jax.experimental.pallas import tpu as pltpu
from jax.sharding import PartitionSpec as P

BLK = 128
TREE = {8: 6, 7: 6, 6: 4, 5: 4, 4: 2, 3: 2, 2: 0, 1: 0}
ORDER = ((8, 7), (6, 5), (4, 3), (2, 1))
FINE = 16
MESH = pl.DeviceIdType.MESH
F32 = jnp.float32
BF16 = jnp.bfloat16


def split(value):
    high = value.astype(BF16)
    low = (value - high.astype(F32)).astype(BF16)
    return high, low


def dot_parts(a, b, dims):
    def one(left, right):
        return lax.dot_general(left, right, (dims, ((), ())), preferred_element_type=F32)

    return one(a[0], b[0]) + (one(a[0], b[1]) + one(a[1], b[0]))


def nn(a, b):
    return dot_parts(split(a), b, ((1,), (0,)))


def nt(a, b):
    return dot_parts(split(a), b, ((1,), (1,)))


def kernel(
    side, pieces,
    in_one_hbm, in_two_hbm, l_one_hbm, l_two_hbm, l_pair_hbm, z_hbm, linv_one_hbm, linv_two_hbm,
    cols_hbm, tiles_hbm,
    in_one, in_two, l_one, l_two, l_pair, z_v, linv_one, linv_two,
    own, hop, far, near, corner, res, m_high, m_low, part, tree, pack, got, cols_v, tiles_v,
    local_sem, hop_recv, far_recv, send_sem, first_recv, second_recv, core_recv, tree_send, tree_recv, got_sem,
):
    chips = side * side
    zn = chips
    width = l_one.shape[1]
    row = lax.axis_index("row")
    col = lax.axis_index("col")
    core = lax.rem(row, 2)
    chip = lax.div(row, 2)
    x = lax.div(chip, side)
    y = lax.rem(chip, side)
    sibling = row + 1 - 2 * core
    here = core * chips + chip

    def send(source, target, s_sem, r_sem, device):
        pltpu.make_async_remote_copy(
            src_ref=source, dst_ref=target, send_sem=s_sem, recv_sem=r_sem,
            device_id=device, device_id_type=MESH,
        ).start()

    def arrived(ref, sem):
        pltpu.make_async_copy(ref, ref, sem).wait()

    staged = [
        pltpu.make_async_copy(source, target, local_sem.at[n])
        for n, (source, target) in enumerate((
            (in_one_hbm, in_one), (in_two_hbm, in_two), (l_one_hbm, l_one), (l_two_hbm, l_two),
            (l_pair_hbm, l_pair), (z_hbm, z_v), (linv_one_hbm, linv_one), (linv_two_hbm, linv_two),
        ))
    ]
    for copy in staged:
        copy.start()

    barrier = pltpu.get_barrier_semaphore()

    def greet(device):
        pl.semaphore_signal(barrier, inc=1, device_id=device, device_id_type=MESH)

    for step in sorted(range(1, zn), key=lambda n: -min(n, zn - n)):
        greet((row, lax.rem(col + step, zn)))
    for step in range(1, chips):
        greet((2 * lax.rem(chip + step, chips) + core, col))
    greet((sibling, col))

    for copy in staged[:5]:
        copy.wait()
    block = lax.div(row * (zn * FINE) + col * FINE, BLK)
    flag_one = in_one[block].astype(F32)
    flag_two = in_two[block].astype(F32)
    mine_one = l_one[...] * flag_one
    mine_two = l_two[...] * flag_two
    near[here, :, :width] = mine_one
    near[here, :, width:2 * width] = mine_two
    corner[here] = l_pair[...]
    tiles = width // 128
    for tile in range(2 * tiles):
        source = mine_one if tile < tiles else mine_two
        at = (tile % tiles) * 128
        for half in range(2):
            own[2 * tile + half] = source[8 * half:8 * half + 8, at:at + 128]

    group = zn // 2
    lead = zn // 4
    depth = zn * FINE

    def place(first, second, which):
        xs = lax.rem(x + side + first * (1 - which) + second * which, side)
        ys = lax.rem(y + side + first * which + second * (1 - which), side)
        return xs * side + ys

    def peer(first, second):
        return (2 * place(first, second, core) + core, col)

    def spread_first(view, sem, which):
        for d in range(1, side):
            send(view(here), view(here), send_sem.at[sem], first_recv.at[which, d], peer(d, 0))

    def spread_second(view, sem, which):
        for e in range(side):
            spot = core * chips + place(-e, 0, core)
            if e:
                arrived(view(spot), first_recv.at[which, e])
            for d in range(1, side):
                send(view(spot), view(spot), send_sem.at[sem], second_recv.at[which, e, d], peer(0, d))
            send(view(spot), view(spot), send_sem.at[sem], core_recv.at[which], (sibling, col))

    def spread_third(view, sem, which):
        for d in range(1, side):
            for e in range(side):
                spot = core * chips + place(-e, -d, core)
                arrived(view(spot), second_recv.at[which, e, d])
                send(view(spot), view(spot), send_sem.at[sem], core_recv.at[which], (sibling, col))

    def spread_end(view, which):
        arrived(view(pl.ds((1 - core) * chips, chips)), core_recv.at[which])

    def far_half(n):
        return lambda spot: far.at[spot, pl.ds(n * group, group)]

    def near_all(spot):
        return near.at[spot]

    def corner_all(spot):
        return corner.at[spot]

    def res_half(n):
        return lambda spot: res.at[n, spot]

    pl.semaphore_wait(barrier, chips + zn - 1)

    mine = pltpu.make_async_copy(own.at[chip], hop.at[chip], hop_recv.at[chip])
    mine.start()
    for step in range(1, chips):
        to = lax.rem(chip + step, chips)
        send(own.at[to], hop.at[chip], send_sem.at[0], hop_recv.at[chip], (2 * to + core, col))
    spread_first(near_all, 3, 2)
    spread_first(corner_all, 5, 5)
    staged[5].wait()
    turn = lax.rem(lead * FINE + (zn - col) * FINE, zn * FINE)
    z_parts = split(jnp.concatenate(
        [pltpu.roll(z_v[:, n * depth:(n + 1) * depth], turn, 1) for n in range(2)], axis=1
    ))
    for step in sorted(range(1, zn), key=lambda n: -min(n, zn - n)):
        to = lax.rem(col + step, zn)
        spot = (lead - step) % zn
        arrived(hop.at[to], hop_recv.at[to])
        send(hop.at[to], far.at[here, spot], send_sem.at[1], far_recv.at[spot // group], (row, to))
    arrived(hop.at[col], hop_recv.at[col])
    far[here, lead] = hop[col]
    spread_second(near_all, 3, 2)

    arrived(far.at[0, pl.ds(0, group - 1)], far_recv.at[0])
    spread_first(far_half(0), 2, 0)
    arrived(far.at[0, pl.ds(0, group)], far_recv.at[1])
    spread_first(far_half(1), 2, 1)
    spread_second(far_half(0), 2, 0)
    spread_second(far_half(1), 2, 1)
    spread_third(near_all, 3, 2)
    spread_third(far_half(0), 2, 0)
    spread_third(far_half(1), 2, 1)
    spread_end(far_half(0), 0)
    spread_second(corner_all, 5, 5)
    spread_end(far_half(1), 1)

    for which in range(2):
        for tile in range(2 * tiles):
            at = which * chips + 2 * tile
            value = jnp.stack([far[at], far[at + 1]], axis=1).reshape(depth, 128)
            high, low = split(value)
            rows = slice(which * depth, (which + 1) * depth)
            m_high[rows, tile * 128:tile * 128 + 128] = high
            m_low[rows, tile * 128:tile * 128 + 128] = low

    most = zn // 2
    ways = (0, 1)
    above = {d: TREE.get(d, 0) for d in range(1, most + 1)}

    def reach(piece, way):
        return most if (piece + way) % 2 == 0 else most - 1

    def along(way, distance):
        return lax.rem(col + (distance if way == 0 else zn - distance), zn)

    def gathered(piece, way, distance):
        total = part[piece, along(way, distance)] if distance else None
        for d in range(reach(piece, way), 0, -1):
            if above[d] == distance:
                arrived(tree.at[piece, way, d - 1], tree_recv.at[piece, way, d - 1])
                value = tree[piece, way, d - 1]
                total = value if total is None else total + value
        return total

    def pass_on(piece, way, distance):
        last = reach(piece, way)
        if distance > last:
            return
        below = [d for d in range(1, last + 1) if above[d] == distance]
        if below:
            tree[piece, way, below[0] - 1] = gathered(piece, way, distance)
            source = tree.at[piece, way, below[0] - 1]
        else:
            source = part.at[piece, along(way, distance)]
        send(source, tree.at[piece, way, distance - 1], tree_send.at[piece, way], tree_recv.at[piece, way, distance - 1],
             (row, along(way, distance - above[distance])))

    share = 2 * width // pieces
    turns = [[d for d in group if d <= most] for group in ORDER]
    turns = [group for group in turns if group]
    for piece in range(pieces):
        cols = slice(piece * share, (piece + 1) * share)
        product = dot_parts(z_parts, (m_high[:, cols], m_low[:, cols]), ((1,), (0,)))
        part[piece] = product.reshape(zn, FINE, share)
        for way in ways:
            for distance in turns[0]:
                pass_on(piece, way, distance)
    for n, group in enumerate(turns[1:]):
        for piece in range(pieces):
            for way in ways:
                for distance in group:
                    pass_on(piece, way, distance)
        if n == 1:
            spread_third(corner_all, 5, 5)
    if len(turns) < 3:
        spread_third(corner_all, 5, 5)

    for copy in staged[6:]:
        copy.wait()
    inv_one = split(linv_one[...])
    inv_two = split(linv_two[...])
    spread_end(near_all, 2)
    spread_end(corner_all, 5)
    count = 2 * chips * FINE
    near_one = split(near[:, :, :width].reshape(count, width))
    near_two = split(near[:, :, width:2 * width].reshape(count, width))
    pair = jnp.concatenate(
        [corner[which * chips + t] for t in range(chips) for which in range(2)], axis=0
    )
    pair = split(pair)
    line = lax.broadcasted_iota(jnp.int32, (48, width), 0)
    lane = lax.broadcasted_iota(jnp.int32, (48, width), 1)
    wanted = jnp.where(line < 16, row * 16 + line, col * 32 + line - 16)
    pick = jnp.where(lane == wanted, 1.0, 0.0).astype(F32)
    tri_one = nt(pick, inv_one)
    tri_two = nt(pick, inv_two)
    tri_pair = nt(nt(tri_two, pair), inv_one)
    u_one_t = nt(tri_one[:16], near_one)
    u_two_t = nt(tri_two[:16], near_two)
    q_t = nt(tri_pair[:16], near_one)
    gram_one = nt(tri_one[:16], split(tri_one[16:]))
    gram_pair = nt(tri_one[:16], split(tri_pair[16:]))
    gram_two = nt(tri_two[:16], split(tri_two[16:])) + nt(tri_pair[:16], split(tri_pair[16:]))

    for piece in range(pieces):
        sums = [gathered(piece, way, 0) for way in ways]
        at = piece * share % width
        n = piece * share // width
        res[n, here, :, at:at + share] = part[piece, col] + sums[0] + sums[1]
        if at + share == width:
            spread_first(res_half(n), 4, 3 + n)

    y_one = nn(res[0, here], inv_one)
    one = -(flag_one * y_one)
    cols_v[0] = one
    spread_second(res_half(0), 4, 3)
    spread_second(res_half(1), 4, 4)
    y_two = nn(res[1, here] + nn(one, pair), inv_two)
    cols_v[1] = -(flag_two * y_two)
    written = pltpu.make_async_copy(cols_v, cols_hbm, local_sem.at[0])
    written.start()
    spread_third(res_half(0), 4, 3)
    spread_third(res_half(1), 4, 4)
    spread_end(res_half(0), 3)

    res_one = split(res[0].reshape(count, width))
    a = nn(jnp.concatenate([u_one_t, u_two_t, q_t], axis=0), res_one)
    y_t = nt(jnp.concatenate([tri_one[:16], tri_pair[:16]], axis=0), res_one)
    c = nn(y_t, near_two)
    d = nn(jnp.concatenate([a[:16], a[32:] - a[16:32]], axis=0), inv_one)
    e = nn(d, pair)
    spread_end(res_half(1), 4)
    b = nn(u_two_t, split(res[1].reshape(count, width)))
    s = nn(e + jnp.concatenate([-c[:16], b - c[16:]], axis=0), inv_two)
    sums = (d[:16], s[:16], s[16:])

    lanes = lax.broadcasted_iota(jnp.int32, (FINE, 128), 1)
    for owner in range(zn):
        at = (owner // 4) * 128
        packed = jnp.zeros((FINE, 128), F32)
        for n in range(3):
            piece = sums[n][:, at:at + 128]
            shift = (32 * n - 32 * (owner % 4)) % 128
            if shift:
                piece = pltpu.roll(piece, shift, 1)
            packed = jnp.where((lanes >= 32 * n) & (lanes < 32 * n + 32), piece, packed)
        pack[owner] = packed
    for step in sorted(range(1, zn), key=lambda n: -min(n, zn - n)):
        to = lax.rem(col + step, zn)
        send(pack.at[to], got.at[step], got_sem.at[0], got_sem.at[1], (row, to))
    arrived(got.at[pl.ds(1, zn - 1)], got_sem.at[1])
    total = pack[col]
    for step in range(1, zn):
        total = total + got[step]
    grams = jnp.concatenate([gram_one, gram_pair, gram_two, jnp.zeros((FINE, 32), F32)], axis=1)
    total = total + grams
    tiles_v[...] = jnp.where((lanes >= 32) & (lanes < 64), -total, total)
    ended = pltpu.make_async_copy(tiles_v, tiles_hbm, local_sem.at[1])
    ended.start()

    arrived(own.at[pl.ds(0, chips - 1)], send_sem.at[0])
    arrived(hop.at[pl.ds(0, zn - 1)], send_sem.at[1])
    arrived(far.at[pl.ds(0, 2 * chips - 1)], send_sem.at[2])
    arrived(near.at[pl.ds(0, 2 * chips - 1)], send_sem.at[3])
    arrived(corner.at[pl.ds(0, 2 * chips - 1)], send_sem.at[5])
    for n in range(2):
        arrived(res.at[n, pl.ds(0, 2 * chips - 1)], send_sem.at[4])
    for piece in range(pieces):
        for way in ways:
            arrived(part.at[piece, pl.ds(0, reach(piece, way))], tree_send.at[piece, way])
    arrived(got.at[pl.ds(1, zn - 1)], got_sem.at[0])
    written.wait()
    ended.wait()


def deal(cols, tiles, col_one, diag_one, col_two, pair_block, diag_two, cols_v, tiles_v, out_v, sem):
    loads = [pltpu.make_async_copy(cols, cols_v, sem.at[0]), pltpu.make_async_copy(tiles, tiles_v, sem.at[1])]
    for copy in loads:
        copy.start()
    loads[1].wait()
    stores = []
    for n, target in enumerate((diag_one, pair_block, diag_two)):
        out_v[n] = tiles_v[:, 32 * n:32 * n + 32]
        stores.append(pltpu.make_async_copy(out_v.at[n], target, sem.at[2 + n]))
        stores[-1].start()
    loads[0].wait()
    for n, target in enumerate((col_one, col_two)):
        stores.append(pltpu.make_async_copy(cols_v.at[n], target, sem.at[5 + n]))
        stores[-1].start()
    for copy in stores:
        copy.wait()


def shards(side, z_anc, in_one, in_two, l_one, l_two, l_pair, linv_one, linv_two):
    width = l_one.shape[1]
    chips = side * side
    zn = chips
    rows, depth = z_anc.shape
    pieces = 4 if width > 128 else 2
    share = 2 * width // pieces
    hbm = pl.BlockSpec(memory_space=pl.ANY)
    dma = pltpu.SemaphoreType.DMA
    out = lambda *shape: jax.ShapeDtypeStruct(shape, F32)
    held = lambda array: pltpu.VMEM(array.shape, array.dtype)
    cols, tiles = pl.pallas_call(
        functools.partial(kernel, side, pieces),
        out_shape=(out(2, FINE, width), out(FINE, 128)),
        in_specs=[hbm] * 8,
        out_specs=[hbm] * 2,
        scratch_shapes=[
            pltpu.SMEM(in_one.shape, in_one.dtype),
            pltpu.SMEM(in_two.shape, in_two.dtype),
            held(l_one), held(l_two), held(l_pair), held(z_anc), held(linv_one), held(linv_two),
            pltpu.VMEM((chips, 8, 128), F32),
            pltpu.VMEM((chips, 8, 128), F32),
            pltpu.VMEM((2 * chips, zn, 8, 128), F32),
            pltpu.VMEM((2 * chips, FINE, 2 * width), F32),
            pltpu.VMEM((2 * chips, FINE, width), F32),
            pltpu.VMEM((2, 2 * chips, FINE, width), F32),
            pltpu.VMEM((depth, 2 * width), BF16),
            pltpu.VMEM((depth, 2 * width), BF16),
            pltpu.VMEM((pieces, zn, FINE, share), F32),
            pltpu.VMEM((pieces, 2, zn // 2, FINE, share), F32),
            pltpu.VMEM((zn, FINE, 128), F32),
            pltpu.VMEM((zn, FINE, 128), F32),
            pltpu.VMEM((2, FINE, width), F32),
            pltpu.VMEM((FINE, 128), F32),
            dma((8,)),
            dma((chips,)),
            dma((2,)),
            dma((6,)),
            dma((6, side)),
            dma((6, side, side)),
            dma((6,)),
            dma((pieces, 2)),
            dma((pieces, 2, zn // 2)),
            dma((2,)),
        ],
        compiler_params=pltpu.CompilerParams(
            collective_id=0, has_side_effects=True, vmem_limit_bytes=63 * 1024 * 1024
        ),
    )(in_one, in_two, l_one, l_two, l_pair, z_anc, linv_one, linv_two)
    return tuple(pl.pallas_call(
        deal,
        out_shape=(
            out(FINE, width), out(16, 32), out(FINE, width), out(16, 32), out(16, 32),
        ),
        in_specs=[hbm] * 2,
        out_specs=[hbm] * 5,
        scratch_shapes=[
            pltpu.VMEM((2, FINE, width), F32), pltpu.VMEM((FINE, 128), F32), pltpu.VMEM((3, 16, 32), F32), dma((7,)),
        ],
    )(cols, tiles))


def solution(mesh):
    side = 1
    while side * side < mesh.shape["col"]:
        side += 1
    placed = (
        P("row", "col"),
        P(),
        P(),
        P(("row", "col"), None),
        P(("row", "col"), None),
        P("row", None),
        P(),
        P(),
    )
    return jax.shard_map(
        functools.partial(shards, side),
        mesh=mesh,
        in_specs=placed,
        out_specs=(
            P(("row", "col"), None),
            P("row", "col"),
            P(("row", "col"), None),
            P("row", "col"),
            P("row", "col"),
        ),
        check_vma=False,
    )
```

```python
import functools

import jax
import jax.numpy as jnp
from jax import lax
from jax.experimental import pallas as pl
from jax.experimental.pallas import tpu as pltpu
from jax.sharding import PartitionSpec as P

BLK = 128
TREE = {8: 6, 7: 6, 6: 4, 5: 4, 4: 2, 3: 2, 2: 0, 1: 0}
ORDER = ((8, 7), (6, 5), (4, 3), (2, 1))
FINE = 16
MESH = pl.DeviceIdType.MESH
F32 = jnp.float32
BF16 = jnp.bfloat16


def split(value):
    high = value.astype(BF16)
    low = (value - high.astype(F32)).astype(BF16)
    return high, low


def dot_parts(a, b, dims):
    def one(left, right):
        return lax.dot_general(left, right, (dims, ((), ())), preferred_element_type=F32)

    return one(a[0], b[0]) + (one(a[0], b[1]) + one(a[1], b[0]))


def nn(a, b):
    return dot_parts(split(a), b, ((1,), (0,)))


def nt(a, b):
    return dot_parts(split(a), b, ((1,), (1,)))


def kernel(
    side, pieces,
    in_one_hbm, in_two_hbm, l_one_hbm, l_two_hbm, l_pair_hbm, z_hbm, linv_one_hbm, linv_two_hbm,
    cols_hbm, tiles_hbm,
    in_one, in_two, l_one, l_two, l_pair, z_v, linv_one, linv_two,
    own, hop, far, near, corner, res, m_high, m_low, part, tree, pack, got, cols_v, tiles_v, told,
    local_sem, hop_recv, far_recv, send_sem, first_recv, second_recv, core_recv, tree_send, tree_recv, got_sem,
):
    chips = side * side
    zn = chips
    width = l_one.shape[1]
    row = lax.axis_index("row")
    col = lax.axis_index("col")
    core = lax.rem(row, 2)
    chip = lax.div(row, 2)
    x = lax.div(chip, side)
    y = lax.rem(chip, side)
    sibling = row + 1 - 2 * core
    here = core * chips + chip

    def send(source, target, s_sem, r_sem, device):
        pltpu.make_async_remote_copy(
            src_ref=source, dst_ref=target, send_sem=s_sem, recv_sem=r_sem,
            device_id=device, device_id_type=MESH,
        ).start()

    def arrived(ref, sem):
        pltpu.make_async_copy(ref, ref, sem).wait()

    staged = [
        pltpu.make_async_copy(source, target, local_sem.at[n])
        for n, (source, target) in enumerate((
            (in_one_hbm, in_one), (in_two_hbm, in_two), (l_one_hbm, l_one), (l_two_hbm, l_two),
            (l_pair_hbm, l_pair), (z_hbm, z_v), (linv_one_hbm, linv_one), (linv_two_hbm, linv_two),
        ))
    ]
    for copy in staged:
        copy.start()

    barrier = pltpu.get_barrier_semaphore()

    def greet(device):
        pl.semaphore_signal(barrier, inc=1, device_id=device, device_id_type=MESH)

    low = row - core
    greet((sibling, col))
    for step in sorted(range(1, zn), key=lambda n: -min(n, zn - n)):
        greet((low, lax.rem(col + step, zn)))
    for step in range(1, chips):
        greet((2 * lax.rem(chip + step, chips) + 1, col))

    def hear(heard, own_part):
        @pl.when(core == own_part)
        def _():
            pl.semaphore_wait(barrier, heard)
            pl.semaphore_signal(told, inc=1, device_id=(sibling, col), device_id_type=MESH)

        @pl.when(core != own_part)
        def _():
            pl.semaphore_wait(told, 1)

    for copy in staged[:5]:
        copy.wait()
    block = lax.div(row * (zn * FINE) + col * FINE, BLK)
    flag_one = in_one[block].astype(F32)
    flag_two = in_two[block].astype(F32)
    mine_one = l_one[...] * flag_one
    mine_two = l_two[...] * flag_two
    near[here, :, :width] = mine_one
    near[here, :, width:2 * width] = mine_two
    corner[here] = l_pair[...]
    tiles = width // 128
    for tile in range(2 * tiles):
        source = mine_one if tile < tiles else mine_two
        at = (tile % tiles) * 128
        for half in range(2):
            own[2 * tile + half] = source[8 * half:8 * half + 8, at:at + 128]

    group = zn // 2
    lead = zn // 4
    depth = zn * FINE

    def place(first, second, which):
        xs = lax.rem(x + side + first * (1 - which) + second * which, side)
        ys = lax.rem(y + side + first * which + second * (1 - which), side)
        return xs * side + ys

    def peer(first, second):
        return (2 * place(first, second, core) + core, col)

    def spread_first(view, sem, which):
        for d in range(1, side):
            send(view(here), view(here), send_sem.at[sem], first_recv.at[which, d], peer(d, 0))

    def spread_second(view, sem, which):
        for e in range(side):
            spot = core * chips + place(-e, 0, core)
            if e:
                arrived(view(spot), first_recv.at[which, e])
            for d in range(1, side):
                send(view(spot), view(spot), send_sem.at[sem], second_recv.at[which, e, d], peer(0, d))
            send(view(spot), view(spot), send_sem.at[sem], core_recv.at[which], (sibling, col))

    def spread_third(view, sem, which):
        for d in range(1, side):
            for e in range(side):
                spot = core * chips + place(-e, -d, core)
                arrived(view(spot), second_recv.at[which, e, d])
                send(view(spot), view(spot), send_sem.at[sem], core_recv.at[which], (sibling, col))

    def spread_end(view, which):
        arrived(view(pl.ds((1 - core) * chips, chips)), core_recv.at[which])

    def far_half(n):
        return lambda spot: far.at[spot, pl.ds(n * group, group)]

    def near_all(spot):
        return near.at[spot]

    def corner_all(spot):
        return corner.at[spot]

    def res_half(n):
        return lambda spot: res.at[n, spot]

    hear(2 * chips - 1, 1)

    mine = pltpu.make_async_copy(own.at[chip], hop.at[chip], hop_recv.at[chip])
    mine.start()
    for step in range(1, chips):
        to = lax.rem(chip + step, chips)
        send(own.at[to], hop.at[chip], send_sem.at[0], hop_recv.at[chip], (2 * to + core, col))
    spread_first(near_all, 3, 2)
    spread_first(corner_all, 5, 5)
    staged[5].wait()
    turn = lax.rem(lead * FINE + (zn - col) * FINE, zn * FINE)
    z_parts = [
        split(pltpu.roll(z_v[:, pl.ds(pl.multiple_of(which * depth, depth), depth)], turn, 1)) for which in (core, 1 - core)
    ]
    hear(2 * zn - 1, 0)
    for step in sorted(range(1, zn), key=lambda n: -min(n, zn - n)):
        to = lax.rem(col + step, zn)
        spot = (lead - step) % zn
        arrived(hop.at[to], hop_recv.at[to])
        send(hop.at[to], far.at[here, spot], send_sem.at[1], far_recv.at[spot // group], (row, to))
    arrived(hop.at[col], hop_recv.at[col])
    far[here, lead] = hop[col]
    spread_second(near_all, 3, 2)

    arrived(far.at[0, pl.ds(0, group - 1)], far_recv.at[0])
    spread_first(far_half(0), 2, 0)
    arrived(far.at[0, pl.ds(0, group)], far_recv.at[1])
    spread_first(far_half(1), 2, 1)
    spread_second(far_half(0), 2, 0)
    spread_second(far_half(1), 2, 1)
    spread_third(near_all, 3, 2)
    spread_third(far_half(0), 2, 0)
    spread_third(far_half(1), 2, 1)
    spread_second(corner_all, 5, 5)

    share = 2 * width // pieces

    def product(n, which):
        for tile in range(2 * tiles):
            at = which * chips + 2 * tile
            value = jnp.stack([far[at], far[at + 1]], axis=1).reshape(depth, 128)
            high, low = split(value)
            m_high[n, :, tile * 128:tile * 128 + 128] = high
            m_low[n, :, tile * 128:tile * 128 + 128] = low

        def of(piece):
            cols = slice(piece * share, (piece + 1) * share)
            value = dot_parts(z_parts[n], (m_high[n, :, cols], m_low[n, :, cols]), ((1,), (0,)))
            return value.reshape(zn, FINE, share)

        return of

    ready = product(0, core)
    for piece in range(pieces):
        part[piece] = ready(piece)
    spread_end(far_half(0), 0)
    spread_end(far_half(1), 1)
    ready = product(1, 1 - core)

    most = zn // 2
    ways = (0, 1)
    above = {d: TREE.get(d, 0) for d in range(1, most + 1)}

    def reach(piece, way):
        return most if (piece + way) % 2 == 0 else most - 1

    def along(way, distance):
        return lax.rem(col + (distance if way == 0 else zn - distance), zn)

    def gathered(piece, way, distance):
        total = part[piece, along(way, distance)] if distance else None
        for d in range(reach(piece, way), 0, -1):
            if above[d] == distance:
                arrived(tree.at[piece, way, d - 1], tree_recv.at[piece, way, d - 1])
                value = tree[piece, way, d - 1]
                total = value if total is None else total + value
        return total

    def pass_on(piece, way, distance):
        last = reach(piece, way)
        if distance > last:
            return
        below = [d for d in range(1, last + 1) if above[d] == distance]
        if below:
            tree[piece, way, below[0] - 1] = gathered(piece, way, distance)
            source = tree.at[piece, way, below[0] - 1]
        else:
            source = part.at[piece, along(way, distance)]
        send(source, tree.at[piece, way, distance - 1], tree_send.at[piece, way], tree_recv.at[piece, way, distance - 1],
             (row, along(way, distance - above[distance])))

    turns = [[d for d in group if d <= most] for group in ORDER]
    turns = [group for group in turns if group]
    for piece in range(pieces):
        part[piece] = part[piece] + ready(piece)
        for way in ways:
            for distance in turns[0]:
                pass_on(piece, way, distance)
    for n, group in enumerate(turns[1:]):
        for piece in range(pieces):
            for way in ways:
                for distance in group:
                    pass_on(piece, way, distance)
        if n == 1:
            spread_third(corner_all, 5, 5)
    if len(turns) < 3:
        spread_third(corner_all, 5, 5)

    for copy in staged[6:]:
        copy.wait()
    inv_one = split(linv_one[...])
    inv_two = split(linv_two[...])
    spread_end(near_all, 2)
    spread_end(corner_all, 5)
    count = 2 * chips * FINE
    near_one = split(near[:, :, :width].reshape(count, width))
    near_two = split(near[:, :, width:2 * width].reshape(count, width))
    pair = jnp.concatenate(
        [corner[which * chips + t] for t in range(chips) for which in range(2)], axis=0
    )
    pair = split(pair)
    line = lax.broadcasted_iota(jnp.int32, (48, width), 0)
    lane = lax.broadcasted_iota(jnp.int32, (48, width), 1)
    wanted = jnp.where(line < 16, row * 16 + line, col * 32 + line - 16)
    pick = jnp.where(lane == wanted, 1.0, 0.0).astype(F32)
    tri_one = nt(pick, inv_one)
    tri_two = nt(pick, inv_two)
    tri_pair = nt(nt(tri_two, pair), inv_one)
    u_one_t = nt(tri_one[:16], near_one)
    u_two_t = nt(tri_two[:16], near_two)
    q_t = nt(tri_pair[:16], near_one)
    gram_one = nt(tri_one[:16], split(tri_one[16:]))
    gram_pair = nt(tri_one[:16], split(tri_pair[16:]))
    gram_two = nt(tri_two[:16], split(tri_two[16:])) + nt(tri_pair[:16], split(tri_pair[16:]))

    for piece in range(pieces):
        sums = [gathered(piece, way, 0) for way in ways]
        at = piece * share % width
        n = piece * share // width
        res[n, here, :, at:at + share] = part[piece, col] + sums[0] + sums[1]
        if at + share == width:
            spread_first(res_half(n), 4, 3 + n)

    y_one = nn(res[0, here], inv_one)
    one = -(flag_one * y_one)
    cols_v[0] = one
    spread_second(res_half(0), 4, 3)
    spread_second(res_half(1), 4, 4)
    y_two = nn(res[1, here] + nn(one, pair), inv_two)
    cols_v[1] = -(flag_two * y_two)
    written = pltpu.make_async_copy(cols_v, cols_hbm, local_sem.at[0])
    written.start()
    spread_third(res_half(0), 4, 3)
    spread_third(res_half(1), 4, 4)
    spread_end(res_half(0), 3)

    res_one = split(res[0].reshape(count, width))
    a = nn(jnp.concatenate([u_one_t, u_two_t, q_t], axis=0), res_one)
    y_t = nt(jnp.concatenate([tri_one[:16], tri_pair[:16]], axis=0), res_one)
    c = nn(y_t, near_two)
    d = nn(jnp.concatenate([a[:16], a[32:] - a[16:32]], axis=0), inv_one)
    e = nn(d, pair)
    spread_end(res_half(1), 4)
    b = nn(u_two_t, split(res[1].reshape(count, width)))
    s = nn(e + jnp.concatenate([-c[:16], b - c[16:]], axis=0), inv_two)
    sums = (d[:16], s[:16], s[16:])

    lanes = lax.broadcasted_iota(jnp.int32, (FINE, 128), 1)
    for owner in range(zn):
        at = (owner // 4) * 128
        packed = jnp.zeros((FINE, 128), F32)
        for n in range(3):
            piece = sums[n][:, at:at + 128]
            shift = (32 * n - 32 * (owner % 4)) % 128
            if shift:
                piece = pltpu.roll(piece, shift, 1)
            packed = jnp.where((lanes >= 32 * n) & (lanes < 32 * n + 32), piece, packed)
        pack[owner] = packed
    for step in sorted(range(1, zn), key=lambda n: -min(n, zn - n)):
        to = lax.rem(col + step, zn)
        send(pack.at[to], got.at[step], got_sem.at[0], got_sem.at[1], (row, to))
    arrived(got.at[pl.ds(1, zn - 1)], got_sem.at[1])
    total = pack[col]
    for step in range(1, zn):
        total = total + got[step]
    grams = jnp.concatenate([gram_one, gram_pair, gram_two, jnp.zeros((FINE, 32), F32)], axis=1)
    total = total + grams
    tiles_v[...] = jnp.where((lanes >= 32) & (lanes < 64), -total, total)
    ended = pltpu.make_async_copy(tiles_v, tiles_hbm, local_sem.at[1])
    ended.start()

    arrived(own.at[pl.ds(0, chips - 1)], send_sem.at[0])
    arrived(hop.at[pl.ds(0, zn - 1)], send_sem.at[1])
    arrived(far.at[pl.ds(0, 2 * chips - 1)], send_sem.at[2])
    arrived(near.at[pl.ds(0, 2 * chips - 1)], send_sem.at[3])
    arrived(corner.at[pl.ds(0, 2 * chips - 1)], send_sem.at[5])
    for n in range(2):
        arrived(res.at[n, pl.ds(0, 2 * chips - 1)], send_sem.at[4])
    for piece in range(pieces):
        for way in ways:
            arrived(part.at[piece, pl.ds(0, reach(piece, way))], tree_send.at[piece, way])
    arrived(got.at[pl.ds(1, zn - 1)], got_sem.at[0])
    written.wait()
    ended.wait()


def deal(cols, tiles, col_one, diag_one, col_two, pair_block, diag_two, cols_v, tiles_v, out_v, sem):
    loads = [pltpu.make_async_copy(cols, cols_v, sem.at[0]), pltpu.make_async_copy(tiles, tiles_v, sem.at[1])]
    for copy in loads:
        copy.start()
    loads[1].wait()
    stores = []
    for n, target in enumerate((diag_one, pair_block, diag_two)):
        out_v[n] = tiles_v[:, 32 * n:32 * n + 32]
        stores.append(pltpu.make_async_copy(out_v.at[n], target, sem.at[2 + n]))
        stores[-1].start()
    loads[0].wait()
    for n, target in enumerate((col_one, col_two)):
        stores.append(pltpu.make_async_copy(cols_v.at[n], target, sem.at[5 + n]))
        stores[-1].start()
    for copy in stores:
        copy.wait()


def shards(side, z_anc, in_one, in_two, l_one, l_two, l_pair, linv_one, linv_two):
    width = l_one.shape[1]
    chips = side * side
    zn = chips
    rows, depth = z_anc.shape
    pieces = 4 if width > 128 else 2
    share = 2 * width // pieces
    hbm = pl.BlockSpec(memory_space=pl.ANY)
    dma = pltpu.SemaphoreType.DMA
    out = lambda *shape: jax.ShapeDtypeStruct(shape, F32)
    held = lambda array: pltpu.VMEM(array.shape, array.dtype)
    cols, tiles = pl.pallas_call(
        functools.partial(kernel, side, pieces),
        out_shape=(out(2, FINE, width), out(FINE, 128)),
        in_specs=[hbm] * 8,
        out_specs=[hbm] * 2,
        scratch_shapes=[
            pltpu.SMEM(in_one.shape, in_one.dtype),
            pltpu.SMEM(in_two.shape, in_two.dtype),
            held(l_one), held(l_two), held(l_pair), held(z_anc), held(linv_one), held(linv_two),
            pltpu.VMEM((chips, 8, 128), F32),
            pltpu.VMEM((chips, 8, 128), F32),
            pltpu.VMEM((2 * chips, zn, 8, 128), F32),
            pltpu.VMEM((2 * chips, FINE, 2 * width), F32),
            pltpu.VMEM((2 * chips, FINE, width), F32),
            pltpu.VMEM((2, 2 * chips, FINE, width), F32),
            pltpu.VMEM((2, depth // 2, 2 * width), BF16),
            pltpu.VMEM((2, depth // 2, 2 * width), BF16),
            pltpu.VMEM((pieces, zn, FINE, share), F32),
            pltpu.VMEM((pieces, 2, zn // 2, FINE, share), F32),
            pltpu.VMEM((zn, FINE, 128), F32),
            pltpu.VMEM((zn, FINE, 128), F32),
            pltpu.VMEM((2, FINE, width), F32),
            pltpu.VMEM((FINE, 128), F32),
            pltpu.SemaphoreType.REGULAR,
            dma((8,)),
            dma((chips,)),
            dma((2,)),
            dma((6,)),
            dma((6, side)),
            dma((6, side, side)),
            dma((6,)),
            dma((pieces, 2)),
            dma((pieces, 2, zn // 2)),
            dma((2,)),
        ],
        compiler_params=pltpu.CompilerParams(
            collective_id=0, has_side_effects=True, vmem_limit_bytes=63 * 1024 * 1024
        ),
    )(in_one, in_two, l_one, l_two, l_pair, z_anc, linv_one, linv_two)
    return tuple(pl.pallas_call(
        deal,
        out_shape=(
            out(FINE, width), out(16, 32), out(FINE, width), out(16, 32), out(16, 32),
        ),
        in_specs=[hbm] * 2,
        out_specs=[hbm] * 5,
        scratch_shapes=[
            pltpu.VMEM((2, FINE, width), F32), pltpu.VMEM((FINE, 128), F32), pltpu.VMEM((3, 16, 32), F32), dma((7,)),
        ],
    )(cols, tiles))


def solution(mesh):
    side = 1
    while side * side < mesh.shape["col"]:
        side += 1
    placed = (
        P("row", "col"),
        P(),
        P(),
        P(("row", "col"), None),
        P(("row", "col"), None),
        P("row", None),
        P(),
        P(),
    )
    return jax.shard_map(
        functools.partial(shards, side),
        mesh=mesh,
        in_specs=placed,
        out_specs=(
            P(("row", "col"), None),
            P("row", "col"),
            P(("row", "col"), None),
            P("row", "col"),
            P("row", "col"),
        ),
        check_vma=False,
    )
```

```python
import functools

import jax
import jax.numpy as jnp
from jax import lax
from jax.experimental import pallas as pl
from jax.experimental.pallas import tpu as pltpu
from jax.sharding import PartitionSpec as P

BLK = 128
TREE = {8: 6, 7: 6, 6: 4, 5: 4, 4: 2, 3: 2, 2: 0, 1: 0}
ORDER = ((8, 7), (6, 5), (4, 3), (2, 1))
FINE = 16
MESH = pl.DeviceIdType.MESH
F32 = jnp.float32
BF16 = jnp.bfloat16


def split(value):
    high = value.astype(BF16)
    low = (value - high.astype(F32)).astype(BF16)
    return high, low


def dot_parts(a, b, dims):
    def one(left, right):
        return lax.dot_general(left, right, (dims, ((), ())), preferred_element_type=F32)

    return one(a[0], b[0]) + (one(a[0], b[1]) + one(a[1], b[0]))


def nn(a, b):
    return dot_parts(split(a), b, ((1,), (0,)))


def nt(a, b):
    return dot_parts(split(a), b, ((1,), (1,)))


def kernel(
    side, pieces,
    in_one_hbm, in_two_hbm, l_one_hbm, l_two_hbm, l_pair_hbm, z_hbm, linv_one_hbm, linv_two_hbm,
    cols_v, tiles_v,
    in_one, in_two, l_one, l_two, l_pair, z_v, linv_one, linv_two,
    own, hop, far, near, corner, res, m_high, m_low, part, tree, pack, got, told,
    local_sem, hop_recv, far_recv, send_sem, first_recv, second_recv, core_recv, tree_send, tree_recv, got_sem,
):
    chips = side * side
    zn = chips
    width = l_one.shape[1]
    row = lax.axis_index("row")
    col = lax.axis_index("col")
    core = lax.rem(row, 2)
    chip = lax.div(row, 2)
    x = lax.div(chip, side)
    y = lax.rem(chip, side)
    sibling = row + 1 - 2 * core
    here = core * chips + chip

    def send(source, target, s_sem, r_sem, device):
        pltpu.make_async_remote_copy(
            src_ref=source, dst_ref=target, send_sem=s_sem, recv_sem=r_sem,
            device_id=device, device_id_type=MESH,
        ).start()

    def arrived(ref, sem):
        pltpu.make_async_copy(ref, ref, sem).wait()

    staged = [
        pltpu.make_async_copy(source, target, local_sem.at[n])
        for n, (source, target) in enumerate((
            (in_one_hbm, in_one), (in_two_hbm, in_two), (l_one_hbm, l_one), (l_two_hbm, l_two),
            (l_pair_hbm, l_pair), (z_hbm, z_v), (linv_one_hbm, linv_one), (linv_two_hbm, linv_two),
        ))
    ]
    for copy in staged:
        copy.start()

    barrier = pltpu.get_barrier_semaphore()

    def greet(device):
        pl.semaphore_signal(barrier, inc=1, device_id=device, device_id_type=MESH)

    low = row - core
    greet((sibling, col))
    for step in sorted(range(1, zn), key=lambda n: -min(n, zn - n)):
        greet((low, lax.rem(col + step, zn)))
    for step in range(1, chips):
        greet((2 * lax.rem(chip + step, chips) + 1, col))

    def hear(heard, own_part):
        @pl.when(core == own_part)
        def _():
            pl.semaphore_wait(barrier, heard)
            pl.semaphore_signal(told, inc=1, device_id=(sibling, col), device_id_type=MESH)

        @pl.when(core != own_part)
        def _():
            pl.semaphore_wait(told, 1)

    for copy in staged[:5]:
        copy.wait()
    block = lax.div(row * (zn * FINE) + col * FINE, BLK)
    flag_one = in_one[block].astype(F32)
    flag_two = in_two[block].astype(F32)
    mine_one = l_one[...] * flag_one
    mine_two = l_two[...] * flag_two
    near[here, :, :width] = mine_one
    near[here, :, width:2 * width] = mine_two
    corner[here] = l_pair[...]
    tiles = width // 128
    for tile in range(2 * tiles):
        source = mine_one if tile < tiles else mine_two
        at = (tile % tiles) * 128
        for half in range(2):
            own[2 * tile + half] = source[8 * half:8 * half + 8, at:at + 128]

    group = zn // 2
    lead = zn // 4
    depth = zn * FINE

    def place(first, second, which):
        xs = lax.rem(x + side + first * (1 - which) + second * which, side)
        ys = lax.rem(y + side + first * which + second * (1 - which), side)
        return xs * side + ys

    def peer(first, second):
        return (2 * place(first, second, core) + core, col)

    def spread_first(view, sem, which):
        for d in range(1, side):
            send(view(here), view(here), send_sem.at[sem], first_recv.at[which, d], peer(d, 0))

    def spread_second(view, sem, which):
        for e in range(side):
            spot = core * chips + place(-e, 0, core)
            if e:
                arrived(view(spot), first_recv.at[which, e])
            for d in range(1, side):
                send(view(spot), view(spot), send_sem.at[sem], second_recv.at[which, e, d], peer(0, d))
            send(view(spot), view(spot), send_sem.at[sem], core_recv.at[which], (sibling, col))

    def spread_third(view, sem, which):
        for d in range(1, side):
            for e in range(side):
                spot = core * chips + place(-e, -d, core)
                arrived(view(spot), second_recv.at[which, e, d])
                send(view(spot), view(spot), send_sem.at[sem], core_recv.at[which], (sibling, col))

    def spread_end(view, which):
        arrived(view(pl.ds((1 - core) * chips, chips)), core_recv.at[which])

    def far_half(n):
        return lambda spot: far.at[spot, pl.ds(n * group, group)]

    def near_all(spot):
        return near.at[spot]

    def corner_all(spot):
        return corner.at[spot]

    def res_half(n):
        return lambda spot: res.at[n, spot]

    hear(2 * chips - 1, 1)

    mine = pltpu.make_async_copy(own.at[chip], hop.at[chip], hop_recv.at[chip])
    mine.start()
    for step in range(1, chips):
        to = lax.rem(chip + step, chips)
        send(own.at[to], hop.at[chip], send_sem.at[0], hop_recv.at[chip], (2 * to + core, col))
    staged[5].wait()
    turn = lax.rem(lead * FINE + (zn - col) * FINE, zn * FINE)
    z_parts = [
        split(pltpu.roll(z_v[:, pl.ds(pl.multiple_of(which * depth, depth), depth)], turn, 1)) for which in (core, 1 - core)
    ]
    hear(2 * zn - 1, 0)
    for step in sorted(range(1, zn), key=lambda n: -min(n, zn - n)):
        to = lax.rem(col + step, zn)
        spot = (lead - step) % zn
        arrived(hop.at[to], hop_recv.at[to])
        send(hop.at[to], far.at[here, spot], send_sem.at[1], far_recv.at[spot // group], (row, to))
    arrived(hop.at[col], hop_recv.at[col])
    far[here, lead] = hop[col]
    spread_first(near_all, 3, 2)
    spread_first(corner_all, 5, 5)

    arrived(far.at[0, pl.ds(0, group - 1)], far_recv.at[0])
    spread_first(far_half(0), 2, 0)
    arrived(far.at[0, pl.ds(0, group)], far_recv.at[1])
    spread_first(far_half(1), 2, 1)
    spread_second(far_half(0), 2, 0)
    spread_second(far_half(1), 2, 1)
    spread_third(far_half(0), 2, 0)
    spread_third(far_half(1), 2, 1)
    spread_second(near_all, 3, 2)
    spread_second(corner_all, 5, 5)

    share = 2 * width // pieces

    def product(n, which):
        for tile in range(2 * tiles):
            at = which * chips + 2 * tile
            value = jnp.stack([far[at], far[at + 1]], axis=1).reshape(depth, 128)
            high, low = split(value)
            m_high[n, :, tile * 128:tile * 128 + 128] = high
            m_low[n, :, tile * 128:tile * 128 + 128] = low

        def of(piece):
            cols = slice(piece * share, (piece + 1) * share)
            value = dot_parts(z_parts[n], (m_high[n, :, cols], m_low[n, :, cols]), ((1,), (0,)))
            return value.reshape(zn, FINE, share)

        return of

    ready = product(0, core)
    for piece in range(pieces):
        part[piece] = ready(piece)
    spread_end(far_half(0), 0)
    spread_end(far_half(1), 1)
    ready = product(1, 1 - core)

    most = zn // 2
    ways = (0, 1)
    above = {d: TREE.get(d, 0) for d in range(1, most + 1)}

    def reach(piece, way):
        return most if (piece + way) % 2 == 0 else most - 1

    def along(way, distance):
        return lax.rem(col + (distance if way == 0 else zn - distance), zn)

    def gathered(piece, way, distance):
        total = part[piece, along(way, distance)] if distance else None
        for d in range(reach(piece, way), 0, -1):
            if above[d] == distance:
                arrived(tree.at[piece, way, d - 1], tree_recv.at[piece, way, d - 1])
                value = tree[piece, way, d - 1]
                total = value if total is None else total + value
        return total

    def pass_on(piece, way, distance):
        last = reach(piece, way)
        if distance > last:
            return
        below = [d for d in range(1, last + 1) if above[d] == distance]
        if below:
            tree[piece, way, below[0] - 1] = gathered(piece, way, distance)
            source = tree.at[piece, way, below[0] - 1]
        else:
            source = part.at[piece, along(way, distance)]
        send(source, tree.at[piece, way, distance - 1], tree_send.at[piece, way], tree_recv.at[piece, way, distance - 1],
             (row, along(way, distance - above[distance])))

    turns = [[d for d in group if d <= most] for group in ORDER]
    turns = [group for group in turns if group]
    for piece in range(pieces):
        part[piece] = part[piece] + ready(piece)
        for way in ways:
            for distance in turns[0]:
                pass_on(piece, way, distance)
    for n, group in enumerate(turns[1:]):
        for piece in range(pieces):
            for way in ways:
                for distance in group:
                    pass_on(piece, way, distance)
        if n == 1:
            spread_third(near_all, 3, 2)
            spread_third(corner_all, 5, 5)
    if len(turns) < 3:
        spread_third(near_all, 3, 2)
        spread_third(corner_all, 5, 5)

    for copy in staged[6:]:
        copy.wait()
    inv_one = split(linv_one[...])
    inv_two = split(linv_two[...])
    spread_end(near_all, 2)
    spread_end(corner_all, 5)
    count = 2 * chips * FINE
    near_one = split(near[:, :, :width].reshape(count, width))
    near_two = split(near[:, :, width:2 * width].reshape(count, width))
    pair = jnp.concatenate(
        [corner[which * chips + t] for t in range(chips) for which in range(2)], axis=0
    )
    pair = split(pair)
    line = lax.broadcasted_iota(jnp.int32, (48, width), 0)
    lane = lax.broadcasted_iota(jnp.int32, (48, width), 1)
    wanted = jnp.where(line < 16, row * 16 + line, col * 32 + line - 16)
    pick = jnp.where(lane == wanted, 1.0, 0.0).astype(F32)
    tri_one = nt(pick, inv_one)
    tri_two = nt(pick, inv_two)
    tri_pair = nt(nt(tri_two, pair), inv_one)
    u_one_t = nt(tri_one[:16], near_one)
    u_two_t = nt(tri_two[:16], near_two)
    q_t = nt(tri_pair[:16], near_one)
    gram_one = nt(tri_one[:16], split(tri_one[16:]))
    gram_pair = nt(tri_one[:16], split(tri_pair[16:]))
    gram_two = nt(tri_two[:16], split(tri_two[16:])) + nt(tri_pair[:16], split(tri_pair[16:]))

    for piece in range(pieces):
        sums = [gathered(piece, way, 0) for way in ways]
        at = piece * share % width
        n = piece * share // width
        res[n, here, :, at:at + share] = part[piece, col] + sums[0] + sums[1]
        if at + share == width:
            spread_first(res_half(n), 4, 3 + n)

    y_one = nn(res[0, here], inv_one)
    one = -(flag_one * y_one)
    cols_v[0] = one
    spread_second(res_half(0), 4, 3)
    spread_second(res_half(1), 4, 4)
    y_two = nn(res[1, here] + nn(one, pair), inv_two)
    cols_v[1] = -(flag_two * y_two)
    spread_third(res_half(0), 4, 3)
    spread_third(res_half(1), 4, 4)
    spread_end(res_half(0), 3)

    res_one = split(res[0].reshape(count, width))
    a = nn(jnp.concatenate([u_one_t, u_two_t, q_t], axis=0), res_one)
    y_t = nt(jnp.concatenate([tri_one[:16], tri_pair[:16]], axis=0), res_one)
    c = nn(y_t, near_two)
    d = nn(jnp.concatenate([a[:16], a[32:] - a[16:32]], axis=0), inv_one)
    e = nn(d, pair)
    spread_end(res_half(1), 4)
    b = nn(u_two_t, split(res[1].reshape(count, width)))
    s = nn(e + jnp.concatenate([-c[:16], b - c[16:]], axis=0), inv_two)
    sums = (d[:16], s[:16], s[16:])

    lanes = lax.broadcasted_iota(jnp.int32, (FINE, 128), 1)
    for owner in range(zn):
        at = (owner // 4) * 128
        packed = jnp.zeros((FINE, 128), F32)
        for n in range(3):
            piece = sums[n][:, at:at + 128]
            shift = (32 * n - 32 * (owner % 4)) % 128
            if shift:
                piece = pltpu.roll(piece, shift, 1)
            packed = jnp.where((lanes >= 32 * n) & (lanes < 32 * n + 32), piece, packed)
        pack[owner] = packed
    for step in sorted(range(1, zn), key=lambda n: -min(n, zn - n)):
        to = lax.rem(col + step, zn)
        send(pack.at[to], got.at[step], got_sem.at[0], got_sem.at[1], (row, to))
    arrived(got.at[pl.ds(1, zn - 1)], got_sem.at[1])
    total = pack[col]
    for step in range(1, zn):
        total = total + got[step]
    grams = jnp.concatenate([gram_one, gram_pair, gram_two, jnp.zeros((FINE, 32), F32)], axis=1)
    total = total + grams
    tiles_v[...] = jnp.where((lanes >= 32) & (lanes < 64), -total, total)

    arrived(own.at[pl.ds(0, chips - 1)], send_sem.at[0])
    arrived(hop.at[pl.ds(0, zn - 1)], send_sem.at[1])
    arrived(far.at[pl.ds(0, 2 * chips - 1)], send_sem.at[2])
    arrived(near.at[pl.ds(0, 2 * chips - 1)], send_sem.at[3])
    arrived(corner.at[pl.ds(0, 2 * chips - 1)], send_sem.at[5])
    for n in range(2):
        arrived(res.at[n, pl.ds(0, 2 * chips - 1)], send_sem.at[4])
    for piece in range(pieces):
        for way in ways:
            arrived(part.at[piece, pl.ds(0, reach(piece, way))], tree_send.at[piece, way])
    arrived(got.at[pl.ds(1, zn - 1)], got_sem.at[0])


def deal(cols, tiles, col_one, diag_one, col_two, pair_block, diag_two, out_v, sem):
    stores = []
    for n, target in enumerate((col_one, col_two)):
        stores.append(pltpu.make_async_copy(cols.at[n], target, sem.at[n]))
        stores[-1].start()
    for n, target in enumerate((diag_one, pair_block, diag_two)):
        out_v[n] = tiles[:, 32 * n:32 * n + 32]
        stores.append(pltpu.make_async_copy(out_v.at[n], target, sem.at[2 + n]))
        stores[-1].start()
    for copy in stores:
        copy.wait()


def shards(side, z_anc, in_one, in_two, l_one, l_two, l_pair, linv_one, linv_two):
    width = l_one.shape[1]
    chips = side * side
    zn = chips
    rows, depth = z_anc.shape
    pieces = 4 if width > 128 else 2
    share = 2 * width // pieces
    hbm = pl.BlockSpec(memory_space=pl.ANY)
    vmem = pl.BlockSpec(memory_space=pltpu.VMEM)
    dma = pltpu.SemaphoreType.DMA
    out = lambda *shape: jax.ShapeDtypeStruct(shape, F32)
    held = lambda array: pltpu.VMEM(array.shape, array.dtype)
    cols, tiles = pl.pallas_call(
        functools.partial(kernel, side, pieces),
        out_shape=(pltpu.VMEM((2, FINE, width), F32), pltpu.VMEM((FINE, 128), F32)),
        in_specs=[pl.BlockSpec(memory_space=pltpu.HBM)] * 8,
        out_specs=[vmem] * 2,
        scratch_shapes=[
            pltpu.SMEM(in_one.shape, in_one.dtype),
            pltpu.SMEM(in_two.shape, in_two.dtype),
            held(l_one), held(l_two), held(l_pair), held(z_anc), held(linv_one), held(linv_two),
            pltpu.VMEM((chips, 8, 128), F32),
            pltpu.VMEM((chips, 8, 128), F32),
            pltpu.VMEM((2 * chips, zn, 8, 128), F32),
            pltpu.VMEM((2 * chips, FINE, 2 * width), F32),
            pltpu.VMEM((2 * chips, FINE, width), F32),
            pltpu.VMEM((2, 2 * chips, FINE, width), F32),
            pltpu.VMEM((2, depth // 2, 2 * width), BF16),
            pltpu.VMEM((2, depth // 2, 2 * width), BF16),
            pltpu.VMEM((pieces, zn, FINE, share), F32),
            pltpu.VMEM((pieces, 2, zn // 2, FINE, share), F32),
            pltpu.VMEM((zn, FINE, 128), F32),
            pltpu.VMEM((zn, FINE, 128), F32),
            pltpu.SemaphoreType.REGULAR,
            dma((8,)),
            dma((chips,)),
            dma((2,)),
            dma((6,)),
            dma((6, side)),
            dma((6, side, side)),
            dma((6,)),
            dma((pieces, 2)),
            dma((pieces, 2, zn // 2)),
            dma((2,)),
        ],
        compiler_params=pltpu.CompilerParams(
            collective_id=0, has_side_effects=True, vmem_limit_bytes=63 * 1024 * 1024
        ),
    )(in_one, in_two, l_one, l_two, l_pair, z_anc, linv_one, linv_two)
    return tuple(pl.pallas_call(
        deal,
        out_shape=(
            out(FINE, width), out(16, 32), out(FINE, width), out(16, 32), out(16, 32),
        ),
        in_specs=[vmem] * 2,
        out_specs=[hbm] * 5,
        scratch_shapes=[pltpu.VMEM((3, 16, 32), F32), dma((5,))],
        compiler_params=pltpu.CompilerParams(vmem_limit_bytes=4 * 1024 * 1024),
    )(cols, tiles))


def solution(mesh):
    side = 1
    while side * side < mesh.shape["col"]:
        side += 1
    placed = (
        P("row", "col"),
        P(),
        P(),
        P(("row", "col"), None),
        P(("row", "col"), None),
        P("row", None),
        P(),
        P(),
    )
    return jax.shard_map(
        functools.partial(shards, side),
        mesh=mesh,
        in_specs=placed,
        out_specs=(
            P(("row", "col"), None),
            P("row", "col"),
            P(("row", "col"), None),
            P("row", "col"),
            P("row", "col"),
        ),
        check_vma=False,
    )
```

```python
import functools

import jax
import jax.numpy as jnp
from jax import lax
from jax.experimental import pallas as pl
from jax.experimental.pallas import tpu as pltpu
from jax.sharding import PartitionSpec as P

BLK = 128
TREE = {8: 6, 7: 6, 6: 4, 5: 4, 4: 2, 3: 2, 2: 0, 1: 0}
ORDER = ((8, 7), (6, 5), (4, 3), (2, 1))
FINE = 16
MESH = pl.DeviceIdType.MESH
F32 = jnp.float32
BF16 = jnp.bfloat16


def split(value):
    high = value.astype(BF16)
    low = (value - high.astype(F32)).astype(BF16)
    return high, low


def dot_parts(a, b, dims):
    def one(left, right):
        return lax.dot_general(left, right, (dims, ((), ())), preferred_element_type=F32)

    return one(a[0], b[0]) + (one(a[0], b[1]) + one(a[1], b[0]))


def nn(a, b):
    return dot_parts(split(a), b, ((1,), (0,)))


def nt(a, b):
    return dot_parts(split(a), b, ((1,), (1,)))


def kernel(
    side, pieces,
    in_one_hbm, in_two_hbm, l_one_hbm, l_two_hbm, l_pair_hbm, z_hbm, linv_one_hbm, linv_two_hbm,
    cols_v, tiles_v,
    in_one, in_two, l_one, l_two, l_pair, z_v, linv_one, linv_two,
    own, hop, far, near, corner, res, m_high, m_low, part, tree, pack, got, told,
    local_sem, hop_recv, far_recv, send_sem, first_recv, second_recv, core_recv, tree_send, tree_recv, got_sem,
):
    chips = side * side
    zn = chips
    width = l_one.shape[1]
    row = lax.axis_index("row")
    col = lax.axis_index("col")
    core = lax.rem(row, 2)
    chip = lax.div(row, 2)
    x = lax.div(chip, side)
    y = lax.rem(chip, side)
    sibling = row + 1 - 2 * core
    here = core * chips + chip

    def send(source, target, s_sem, r_sem, device):
        pltpu.make_async_remote_copy(
            src_ref=source, dst_ref=target, send_sem=s_sem, recv_sem=r_sem,
            device_id=device, device_id_type=MESH,
        ).start()

    def arrived(ref, sem):
        pltpu.make_async_copy(ref, ref, sem).wait()

    staged = [
        pltpu.make_async_copy(source, target, local_sem.at[n])
        for n, (source, target) in enumerate((
            (in_one_hbm, in_one), (in_two_hbm, in_two), (l_one_hbm, l_one), (l_two_hbm, l_two),
            (l_pair_hbm, l_pair), (z_hbm, z_v), (linv_one_hbm, linv_one), (linv_two_hbm, linv_two),
        ))
    ]
    for copy in staged:
        copy.start()

    barrier = pltpu.get_barrier_semaphore()

    def greet(device):
        pl.semaphore_signal(barrier, inc=1, device_id=device, device_id_type=MESH)

    low = row - core
    greet((sibling, col))
    for step in sorted(range(1, zn), key=lambda n: -min(n, zn - n)):
        greet((low, lax.rem(col + step, zn)))
    for step in range(1, chips):
        greet((2 * lax.rem(chip + step, chips) + 1, col))

    def hear(heard, own_part):
        @pl.when(core == own_part)
        def _():
            pl.semaphore_wait(barrier, heard)
            pl.semaphore_signal(told, inc=1, device_id=(sibling, col), device_id_type=MESH)

        @pl.when(core != own_part)
        def _():
            pl.semaphore_wait(told, 1)

    for copy in staged[:5]:
        copy.wait()
    block = lax.div(row * (zn * FINE) + col * FINE, BLK)
    flag_one = in_one[block].astype(F32)
    flag_two = in_two[block].astype(F32)
    mine_one = l_one[...] * flag_one
    mine_two = l_two[...] * flag_two
    near[here, :, :width] = mine_one
    near[here, :, width:2 * width] = mine_two
    corner[here] = l_pair[...]
    tiles = width // 128
    for tile in range(2 * tiles):
        source = mine_one if tile < tiles else mine_two
        at = (tile % tiles) * 128
        for half in range(2):
            own[2 * tile + half] = source[8 * half:8 * half + 8, at:at + 128]

    group = zn // 2
    lead = zn // 4
    depth = zn * FINE

    def place(first, second, which):
        xs = lax.rem(x + side + first * (1 - which) + second * which, side)
        ys = lax.rem(y + side + first * which + second * (1 - which), side)
        return xs * side + ys

    def peer(first, second):
        return (2 * place(first, second, core) + core, col)

    def spread_first(view, sem, which):
        for d in range(1, side):
            send(view(here), view(here), send_sem.at[sem], first_recv.at[which, d], peer(d, 0))

    def spread_second(view, sem, which):
        for e in range(side):
            spot = core * chips + place(-e, 0, core)
            if e:
                arrived(view(spot), first_recv.at[which, e])
            for d in range(1, side):
                send(view(spot), view(spot), send_sem.at[sem], second_recv.at[which, e, d], peer(0, d))
            send(view(spot), view(spot), send_sem.at[sem], core_recv.at[which], (sibling, col))

    def spread_third(view, sem, which):
        for d in range(1, side):
            for e in range(side):
                spot = core * chips + place(-e, -d, core)
                arrived(view(spot), second_recv.at[which, e, d])
                send(view(spot), view(spot), send_sem.at[sem], core_recv.at[which], (sibling, col))

    def spread_end(view, which):
        arrived(view(pl.ds((1 - core) * chips, chips)), core_recv.at[which])

    def far_half(n):
        return lambda spot: far.at[spot, pl.ds(n * group, group)]

    def near_all(spot):
        return near.at[spot]

    def corner_all(spot):
        return corner.at[spot]

    def res_half(n):
        return lambda spot: res.at[n, spot]

    hear(2 * chips - 1, 1)

    mine = pltpu.make_async_copy(own.at[chip], hop.at[chip], hop_recv.at[chip])
    mine.start()
    for step in range(1, chips):
        to = lax.rem(chip + step, chips)
        send(own.at[to], hop.at[chip], send_sem.at[0], hop_recv.at[chip], (2 * to + core, col))
    staged[5].wait()
    turn = lax.rem(lead * FINE + (zn - col) * FINE, zn * FINE)
    z_parts = [
        split(pltpu.roll(z_v[:, pl.ds(pl.multiple_of(which * depth, depth), depth)], turn, 1)) for which in (core, 1 - core)
    ]
    hear(2 * zn - 1, 0)
    for step in sorted(range(1, zn), key=lambda n: -min(n, zn - n)):
        to = lax.rem(col + step, zn)
        spot = (lead - step) % zn
        arrived(hop.at[to], hop_recv.at[to])
        send(hop.at[to], far.at[here, spot], send_sem.at[1], far_recv.at[spot // group], (row, to))
    arrived(hop.at[col], hop_recv.at[col])
    far[here, lead] = hop[col]
    spread_first(near_all, 3, 2)
    spread_first(corner_all, 5, 5)

    arrived(far.at[0, pl.ds(0, group - 1)], far_recv.at[0])
    spread_first(far_half(0), 2, 0)
    arrived(far.at[0, pl.ds(0, group)], far_recv.at[1])
    spread_first(far_half(1), 2, 1)
    spread_second(far_half(0), 2, 0)
    spread_second(far_half(1), 2, 1)
    spread_third(far_half(0), 2, 0)
    spread_third(far_half(1), 2, 1)
    spread_second(near_all, 3, 2)
    spread_second(corner_all, 5, 5)

    share = 2 * width // pieces

    def product(n, which):
        for tile in range(2 * tiles):
            at = which * chips + 2 * tile
            value = jnp.stack([far[at], far[at + 1]], axis=1).reshape(depth, 128)
            high, low = split(value)
            m_high[n, :, tile * 128:tile * 128 + 128] = high
            m_low[n, :, tile * 128:tile * 128 + 128] = low

        def of(piece):
            cols = slice(piece * share, (piece + 1) * share)
            value = dot_parts(z_parts[n], (m_high[n, :, cols], m_low[n, :, cols]), ((1,), (0,)))
            return value.reshape(zn, FINE, share)

        return of

    ready = product(0, core)
    for piece in range(pieces):
        part[piece] = ready(piece)
    spread_end(far_half(0), 0)
    spread_end(far_half(1), 1)
    ready = product(1, 1 - core)

    most = zn // 2
    ways = (0, 1)
    above = {d: TREE.get(d, 0) for d in range(1, most + 1)}

    def reach(piece, way):
        return most if (piece + way) % 2 == 0 else most - 1

    def along(way, distance):
        return lax.rem(col + (distance if way == 0 else zn - distance), zn)

    def gathered(piece, way, distance):
        total = part[piece, along(way, distance)] if distance else None
        for d in range(reach(piece, way), 0, -1):
            if above[d] == distance:
                arrived(tree.at[piece, way, d - 1], tree_recv.at[piece, way, d - 1])
                value = tree[piece, way, d - 1]
                total = value if total is None else total + value
        return total

    def pass_on(piece, way, distance):
        last = reach(piece, way)
        if distance > last:
            return
        below = [d for d in range(1, last + 1) if above[d] == distance]
        if below:
            tree[piece, way, below[0] - 1] = gathered(piece, way, distance)
            source = tree.at[piece, way, below[0] - 1]
        else:
            source = part.at[piece, along(way, distance)]
        send(source, tree.at[piece, way, distance - 1], tree_send.at[piece, way], tree_recv.at[piece, way, distance - 1],
             (row, along(way, distance - above[distance])))

    turns = [[d for d in group if d <= most] for group in ORDER]
    turns = [group for group in turns if group]
    for piece in range(pieces):
        part[piece] = part[piece] + ready(piece)
        for way in ways:
            for distance in turns[0]:
                pass_on(piece, way, distance)
    for n, group in enumerate(turns[1:]):
        for piece in range(pieces):
            for way in ways:
                for distance in group:
                    pass_on(piece, way, distance)
        if n == 1:
            spread_third(near_all, 3, 2)
            spread_third(corner_all, 5, 5)
    if len(turns) < 3:
        spread_third(near_all, 3, 2)
        spread_third(corner_all, 5, 5)

    for copy in staged[6:]:
        copy.wait()
    inv_one = split(linv_one[...])
    inv_two = split(linv_two[...])
    spread_end(near_all, 2)
    spread_end(corner_all, 5)
    count = 2 * chips * FINE
    near_one = split(near[:, :, :width].reshape(count, width))
    near_two = split(near[:, :, width:2 * width].reshape(count, width))
    pair = jnp.concatenate(
        [corner[which * chips + t] for t in range(chips) for which in range(2)], axis=0
    )
    pair = split(pair)
    line = lax.broadcasted_iota(jnp.int32, (48, width), 0)
    lane = lax.broadcasted_iota(jnp.int32, (48, width), 1)
    wanted = jnp.where(line < 16, row * 16 + line, col * 32 + line - 16)
    pick = jnp.where(lane == wanted, 1.0, 0.0).astype(F32)
    tri_one = nt(pick, inv_one)
    tri_two = nt(pick, inv_two)
    tri_pair = nt(nt(tri_two, pair), inv_one)
    u_one_t = nt(tri_one[:16], near_one)
    u_two_t = nt(tri_two[:16], near_two)
    q_t = nt(tri_pair[:16], near_one)
    gram_one = nt(tri_one[:16], split(tri_one[16:]))
    gram_pair = nt(tri_one[:16], split(tri_pair[16:]))
    gram_two = nt(tri_two[:16], split(tri_two[16:])) + nt(tri_pair[:16], split(tri_pair[16:]))

    for piece in range(pieces):
        sums = [gathered(piece, way, 0) for way in ways]
        at = piece * share % width
        n = piece * share // width
        res[n, here, :, at:at + share] = part[piece, col] + sums[0] + sums[1]
        if at + share == width:
            spread_first(res_half(n), 4, 3 + n)

    y_one = nn(res[0, here], inv_one)
    one = -(flag_one * y_one)
    cols_v[0] = one
    spread_second(res_half(0), 4, 3)
    spread_second(res_half(1), 4, 4)
    y_two = nn(res[1, here] + nn(one, pair), inv_two)
    cols_v[1] = -(flag_two * y_two)
    spread_third(res_half(0), 4, 3)
    spread_third(res_half(1), 4, 4)
    spread_end(res_half(0), 3)

    res_one = split(res[0].reshape(count, width))
    a = nn(jnp.concatenate([u_one_t, u_two_t, q_t], axis=0), res_one)
    y_t = nt(jnp.concatenate([tri_one[:16], tri_pair[:16]], axis=0), res_one)
    c = nn(y_t, near_two)
    d = nn(jnp.concatenate([a[:16], a[32:] - a[16:32]], axis=0), inv_one)
    e = nn(d, pair)
    spread_end(res_half(1), 4)
    b = nn(u_two_t, split(res[1].reshape(count, width)))
    s = nn(e + jnp.concatenate([-c[:16], b - c[16:]], axis=0), inv_two)
    sums = (d[:16], s[:16], s[16:])

    lanes = lax.broadcasted_iota(jnp.int32, (FINE, 128), 1)
    for owner in range(zn):
        at = (owner // 4) * 128
        packed = jnp.zeros((FINE, 128), F32)
        for n in range(3):
            piece = sums[n][:, at:at + 128]
            shift = (32 * n - 32 * (owner % 4)) % 128
            if shift:
                piece = pltpu.roll(piece, shift, 1)
            packed = jnp.where((lanes >= 32 * n) & (lanes < 32 * n + 32), piece, packed)
        rest = jnp.concatenate([pltpu.roll(packed[12:], 96 - 32 * n, 1) for n in range(3)], axis=0)
        pack[owner] = jnp.where(lanes[:12] >= 96, rest, packed[:12])
    for step in sorted(range(1, zn), key=lambda n: -min(n, zn - n)):
        to = lax.rem(col + step, zn)
        send(pack.at[to], got.at[step], got_sem.at[0], got_sem.at[1], (row, to))
    arrived(got.at[pl.ds(1, zn - 1)], got_sem.at[1])
    total = pack[col]
    for step in range(1, zn):
        total = total + got[step]
    grams = jnp.concatenate([gram_one, gram_pair, gram_two, jnp.zeros((FINE, 32), F32)], axis=1)
    rest = jnp.zeros((4, 128), F32)
    for n in range(3):
        piece = pltpu.roll(total[4 * n:4 * n + 4], 32 + 32 * n, 1)
        rest = jnp.where((lanes[:4] >= 32 * n) & (lanes[:4] < 32 * n + 32), piece, rest)
    total = jnp.concatenate([total, rest], axis=0) + grams
    tiles_v[...] = jnp.where((lanes >= 32) & (lanes < 64), -total, total)

    arrived(own.at[pl.ds(0, chips - 1)], send_sem.at[0])
    arrived(hop.at[pl.ds(0, zn - 1)], send_sem.at[1])
    arrived(far.at[pl.ds(0, 2 * chips - 1)], send_sem.at[2])
    arrived(near.at[pl.ds(0, 2 * chips - 1)], send_sem.at[3])
    arrived(corner.at[pl.ds(0, 2 * chips - 1)], send_sem.at[5])
    for n in range(2):
        arrived(res.at[n, pl.ds(0, 2 * chips - 1)], send_sem.at[4])
    for piece in range(pieces):
        for way in ways:
            arrived(part.at[piece, pl.ds(0, reach(piece, way))], tree_send.at[piece, way])
    arrived(got.at[pl.ds(1, zn - 1)], got_sem.at[0])


def deal(cols, tiles, col_one, diag_one, col_two, pair_block, diag_two, out_v, sem):
    stores = []
    for n, target in enumerate((col_one, col_two)):
        stores.append(pltpu.make_async_copy(cols.at[n], target, sem.at[n]))
        stores[-1].start()
    for n, target in enumerate((diag_one, pair_block, diag_two)):
        out_v[n] = tiles[:, 32 * n:32 * n + 32]
        stores.append(pltpu.make_async_copy(out_v.at[n], target, sem.at[2 + n]))
        stores[-1].start()
    for copy in stores:
        copy.wait()


def shards(side, z_anc, in_one, in_two, l_one, l_two, l_pair, linv_one, linv_two):
    width = l_one.shape[1]
    chips = side * side
    zn = chips
    rows, depth = z_anc.shape
    pieces = 4 if width > 128 else 2
    share = 2 * width // pieces
    hbm = pl.BlockSpec(memory_space=pl.ANY)
    vmem = pl.BlockSpec(memory_space=pltpu.VMEM)
    dma = pltpu.SemaphoreType.DMA
    out = lambda *shape: jax.ShapeDtypeStruct(shape, F32)
    held = lambda array: pltpu.VMEM(array.shape, array.dtype)
    cols, tiles = pl.pallas_call(
        functools.partial(kernel, side, pieces),
        out_shape=(pltpu.VMEM((2, FINE, width), F32), pltpu.VMEM((FINE, 128), F32)),
        in_specs=[pl.BlockSpec(memory_space=pltpu.HBM)] * 8,
        out_specs=[vmem] * 2,
        scratch_shapes=[
            pltpu.SMEM(in_one.shape, in_one.dtype),
            pltpu.SMEM(in_two.shape, in_two.dtype),
            held(l_one), held(l_two), held(l_pair), held(z_anc), held(linv_one), held(linv_two),
            pltpu.VMEM((chips, 8, 128), F32),
            pltpu.VMEM((chips, 8, 128), F32),
            pltpu.VMEM((2 * chips, zn, 8, 128), F32),
            pltpu.VMEM((2 * chips, FINE, 2 * width), F32),
            pltpu.VMEM((2 * chips, FINE, width), F32),
            pltpu.VMEM((2, 2 * chips, FINE, width), F32),
            pltpu.VMEM((2, depth // 2, 2 * width), BF16),
            pltpu.VMEM((2, depth // 2, 2 * width), BF16),
            pltpu.VMEM((pieces, zn, FINE, share), F32),
            pltpu.VMEM((pieces, 2, zn // 2, FINE, share), F32),
            pltpu.VMEM((zn, 12, 128), F32),
            pltpu.VMEM((zn, 12, 128), F32),
            pltpu.SemaphoreType.REGULAR,
            dma((8,)),
            dma((chips,)),
            dma((2,)),
            dma((6,)),
            dma((6, side)),
            dma((6, side, side)),
            dma((6,)),
            dma((pieces, 2)),
            dma((pieces, 2, zn // 2)),
            dma((2,)),
        ],
        compiler_params=pltpu.CompilerParams(
            collective_id=0, has_side_effects=True, vmem_limit_bytes=63 * 1024 * 1024
        ),
    )(in_one, in_two, l_one, l_two, l_pair, z_anc, linv_one, linv_two)
    return tuple(pl.pallas_call(
        deal,
        out_shape=(
            out(FINE, width), out(16, 32), out(FINE, width), out(16, 32), out(16, 32),
        ),
        in_specs=[vmem] * 2,
        out_specs=[hbm] * 5,
        scratch_shapes=[pltpu.VMEM((3, 16, 32), F32), dma((5,))],
        compiler_params=pltpu.CompilerParams(vmem_limit_bytes=4 * 1024 * 1024),
    )(cols, tiles))


def solution(mesh):
    side = 1
    while side * side < mesh.shape["col"]:
        side += 1
    placed = (
        P("row", "col"),
        P(),
        P(),
        P(("row", "col"), None),
        P(("row", "col"), None),
        P("row", None),
        P(),
        P(),
    )
    return jax.shard_map(
        functools.partial(shards, side),
        mesh=mesh,
        in_specs=placed,
        out_specs=(
            P(("row", "col"), None),
            P("row", "col"),
            P(("row", "col"), None),
            P("row", "col"),
            P("row", "col"),
        ),
        check_vma=False,
    )
```
